32 devices in a mesh: tile: 8 (over y, x, core), knot: 4 (over z).
Axes of the slice: x: 2, y: 2, z: 4, core: 2. Of those that a mesh axis runs over, the one named last changes fastest.
Arguments:
- images: float32 [8, 32, 65536], P('tile', 'knot'), may hold values from -6 to 6
- gradient: float32 [8, 32, 65536], P('tile', 'knot'), may hold values from -3 to 3
- shifts: int32 [8], P('tile'), may hold values from -4 to 4
- tile_blocks: int32 [8, 2], P('tile'), may hold values from 0 to 31, as said below
- intersections: int32 [8, 3, 8, 5], P('tile'), may hold values from 0 to 57344, as said below
- start_coefficients: float32 [32, 64], P(('tile', 'knot')), may hold values from -0.6 to 0.6
Outputs:
- coefficients: float32 [32, 64], P(('tile', 'knot'))
- warped: float32 [8, 32, 65536], P('tile', 'knot')
The draws below stay inside these ranges and needn't reach their ends.
Inputs may be any that keep to these rules, and one draw needn't show every extreme that they name: intersections[s, d, m] holds the sending tile's index among the 1 tiles of owner s, its slab offset, the receiving tile's index among the tiles of owner s + d - 1, its slab offset, and a live flag; live slots of one sender and direction come first; no live slot points outside the owners; some owner receives 8 live slots from each of its three senders, and some sender fills 8 slots of a direction. `tile_blocks`: the blocks of a tile held by tile owner i are owned by tile owners i - 1, i or i + 1, block b being owned by device b div 1 in the order of tile and knot joined.
All inputs are finite; a program needn't handle non-finite values.
Results may differ from the reference program's by a relative error of at most 0.0003.
Values sent between devices are 32-bit elements; how exact they have to be, the bound alone decides.
A program may use at most 576 MiB of HBM per device.

```python
import jax
import jax.numpy as jnp
from jax import lax

TILE_DEV = 1
PLANE = 65536
SLAB = 8192
CAP = 8
BLOCK = 64
ITERS = 2
TILES = 8
Z = 32
KNOT_BLOCKS = 32


def draw_tile_blocks(key, part):
    key = jax.random.fold_in(key, 11)
    owners = TILES // TILE_DEV
    width = KNOT_BLOCKS // owners
    home = jnp.arange(TILES, dtype=jnp.int32) // TILE_DEV
    low = jnp.maximum(home - 1, 0) * width
    high = jnp.minimum(home + 2, owners) * width
    picked = jax.random.randint(key, (TILES, 2), low[:, None], high[:, None], dtype=jnp.int32)
    picked = picked.at[0, 0].set(0)
    return picked.at[TILES - 1, 1].set(KNOT_BLOCKS - 1)


def draw_intersections(key, part):
    key = jax.random.fold_in(key, 23)
    owners = TILES // TILE_DEV
    keys = jax.random.split(key, 6)
    shape = (owners, 3, CAP)
    src_tile = jax.random.randint(keys[0], shape, 0, TILE_DEV, dtype=jnp.int32)
    src_off = jax.random.randint(keys[1], shape, 0, PLANE - SLAB + 1, dtype=jnp.int32)
    dst_tile = jax.random.randint(keys[2], shape, 0, TILE_DEV, dtype=jnp.int32)
    dst_off = jax.random.randint(keys[3], shape, 0, PLANE - SLAB + 1, dtype=jnp.int32)
    src_off = src_off.at[0, 1, 0].set(PLANE - SLAB)
    count = jax.random.randint(keys[4], (owners, 3), 1, CAP + 1, dtype=jnp.int32)
    chosen = jax.random.randint(keys[5], (), 1, owners - 1, dtype=jnp.int32)
    rows = jnp.arange(owners, dtype=jnp.int32)[:, None]
    dirs = jnp.arange(3, dtype=jnp.int32)[None, :]
    target = rows + dirs - 1
    count = jnp.where(target == chosen, CAP, count)
    count = jnp.where((target < 0) | (target >= owners), 0, count)
    live = (jnp.arange(CAP, dtype=jnp.int32)[None, None, :] < count[:, :, None]).astype(jnp.int32)
    return jnp.stack([src_tile, src_off, dst_tile, dst_off, live], axis=-1)


def plant(array, own_key, low, top_value):
    longest = array.shape.index(max(array.shape))
    spots = []
    for shift in (0, 1):
        where = [jax.random.randint(jax.random.fold_in(own_key, axis), (), 0, length) for axis, length in enumerate(array.shape)]
        where[longest] = (where[longest] + shift) % array.shape[longest]
        spots.append(tuple(where))
    return array.at[spots[0]].set(low).at[spots[1]].set(top_value)


def shard_levels(stream_key, shape, pieces, least, high):
    def one(dim, shards_of):
        steps = jax.random.uniform(jax.random.fold_in(jax.random.fold_in(stream_key, 6), dim), (shards_of,), jnp.float32, least / len(pieces), high / len(pieces))
        return jnp.repeat(jnp.exp(steps), shape[dim] // shards_of).reshape((-1,) + (1,) * (len(shape) - dim - 1))

    factor_of = one(*pieces[0])
    for cut in pieces[1:]:
        factor_of = factor_of * one(*cut)
    return factor_of


def noise(key, dims, scale, reach, pieces=(), kind=jnp.bfloat16):
    gain = shard_levels(key, dims, pieces, -0.22, 0.18) if pieces else 1.0
    result = jax.random.normal(key, dims, jnp.float32) * scale * gain
    return jnp.minimum(jnp.maximum(result, -reach), reach).astype(kind)


def setup_inputs(seed: int = 0) -> dict:
    seeds = jax.random.split(jax.random.key(seed), 7)
    images = noise(seeds[0], (TILES, Z, PLANE), 1.0, 6.0, ((0, 8), (1, 4)), jnp.float32)
    gradient = noise(seeds[1], (TILES, Z, PLANE), 0.5, 3.0, ((0, 8), (1, 4)), jnp.float32)
    shifts = plant(jax.random.randint(seeds[2], (TILES,), -4, 5), jax.random.fold_in(seeds[2], 1), -4, 4).astype(jnp.int32)
    tile_blocks = draw_tile_blocks(jax.random.fold_in(seeds[6], 71), 0)
    intersections = draw_intersections(jax.random.fold_in(seeds[6], 71), 0)
    start_coefficients = noise(seeds[5], (KNOT_BLOCKS, BLOCK), 0.1, 0.6, ((0, 32),), jnp.float32)
    return dict(images=images, gradient=gradient, shifts=shifts, tile_blocks=tile_blocks, intersections=intersections, start_coefficients=start_coefficients)


shift_step = 0.05
smooth_weight = 20.0
ridge_weight = 1.0

def spline_basis(plane, knots):
    place = jnp.arange(plane, dtype=jnp.float32) * ((knots - 3) / plane) + 1.0
    offset = place[None, :] - jnp.arange(knots, dtype=jnp.float32)[:, None]
    dist = jnp.abs(offset)
    inner = 2.0 / 3.0 - dist * dist + 0.5 * dist * dist * dist
    outer = (2.0 - dist) * (2.0 - dist) * (2.0 - dist) / 6.0
    return jnp.where(dist < 1.0, inner, jnp.where(dist < 2.0, outer, 0.0))

def smoothing(block):
    rows = jnp.arange(block - 2, dtype=jnp.int32)[:, None]
    cols = jnp.arange(block, dtype=jnp.int32)[None, :]
    second = (cols == rows).astype(jnp.float32) - 2.0 * (cols == rows + 1).astype(jnp.float32) + (cols == rows + 2).astype(jnp.float32)
    return jnp.dot(second.T, second, precision=lax.Precision.HIGHEST)

def block_update(normal, gradsum, coef, penalty):
    size = normal.shape[-1]
    system = normal + smooth_weight * penalty + ridge_weight * jnp.eye(size, dtype=jnp.float32)
    pull = jnp.einsum('kl,bl->bk', penalty, coef, precision=lax.Precision.HIGHEST)
    target = -(gradsum + smooth_weight * pull)
    factor = lax.linalg.cholesky(system)
    middle = lax.linalg.triangular_solve(factor, target[..., None], left_side=True, lower=True)
    update = lax.linalg.triangular_solve(factor, middle, left_side=True, lower=True, transpose_a=True)
    return coef + update[..., 0]

def warp_tiles(images, gradient, shifts, tile_blocks, coef, basis):
    local = coef[tile_blocks].reshape(tile_blocks.shape[0], -1)
    field = jnp.dot(local, basis, precision=lax.Precision.HIGHEST)
    offset = field + shift_step * shifts.astype(jnp.float32)[:, None]
    return images + gradient * offset[:, None, :]

def reference(images, gradient, shifts, tile_blocks, intersections, start_coefficients):
    basis = spline_basis(PLANE, 2 * BLOCK)
    penalty = smoothing(BLOCK)
    senders = intersections.shape[0]
    source = jnp.arange(senders, dtype=jnp.int32)[:, None, None]
    receiver = jnp.clip(source + jnp.arange(3, dtype=jnp.int32)[None, :, None] - 1, 0, senders - 1)
    tile_b = (source * TILE_DEV + intersections[..., 0]).reshape(-1).astype(jnp.int32)
    off_b = intersections[..., 1].reshape(-1).astype(jnp.int32)
    tile_a = (receiver * TILE_DEV + intersections[..., 2]).reshape(-1).astype(jnp.int32)
    off_a = intersections[..., 3].reshape(-1).astype(jnp.int32)
    alive = intersections[..., 4].reshape(-1).astype(jnp.float32)
    zero = jnp.zeros((), jnp.int32)
    targets = tile_blocks[tile_a].reshape(-1)
    coef = start_coefficients
    for step in range(ITERS):
        tiles = warp_tiles(images, gradient, shifts, tile_blocks, coef, basis)

        def pair_terms(item):
            tb, ob, ta, oa, live = item
            far = lax.dynamic_slice(tiles, (tb, zero, ob), (1, Z, SLAB))[0]
            near = lax.dynamic_slice(tiles, (ta, zero, oa), (1, Z, SLAB))[0]
            slope = lax.dynamic_slice(gradient, (ta, zero, oa), (1, Z, SLAB))[0]
            misfit = (near - far) * live
            weight = jnp.sum(slope * slope, axis=0) * live
            project = jnp.sum(slope * misfit, axis=0)
            piece = lax.dynamic_slice(basis, (zero, oa), (2 * BLOCK, SLAB)).reshape(2, BLOCK, SLAB)
            normal = jnp.einsum('nks,nls->nkl', piece * weight[None, None, :], piece, precision=lax.Precision.HIGHEST)
            grads = jnp.einsum('nks,s->nk', piece, project, precision=lax.Precision.HIGHEST)
            return (normal, grads)
        normals, grads = lax.map(pair_terms, (tile_b, off_b, tile_a, off_a, alive))
        normal_sum = jnp.zeros((KNOT_BLOCKS, BLOCK, BLOCK), jnp.float32).at[targets].add(normals.reshape(-1, BLOCK, BLOCK))
        grad_sum = jnp.zeros((KNOT_BLOCKS, BLOCK), jnp.float32).at[targets].add(grads.reshape(-1, BLOCK))
        coef = block_update(normal_sum, grad_sum, coef, penalty)
    warped = warp_tiles(images, gradient, shifts, tile_blocks, coef, basis)
    return (coef, warped)
```

```python
import functools

import jax
import jax.numpy as jnp
import numpy as np
from jax import lax
from jax.experimental import pallas as pl
from jax.experimental.pallas import tpu as pltpu
from jax.sharding import PartitionSpec as P

SLAB = 8192
ITERS = 2
LANES = 128
SUB = 8
GROUP = SUB * LANES
FRONT = 8
BACK = 16
WINDOW = 6
BAND = 4
SPAN = SLAB // GROUP + 1

shift_step = 0.05
smooth_weight = 20.0
ridge_weight = 1.0
HIGHEST = lax.Precision.HIGHEST
MESH = pl.DeviceIdType.MESH
VMEM = pl.BlockSpec(memory_space=pltpu.VMEM)
SMEM = pl.BlockSpec(memory_space=pltpu.SMEM)
PARAMS = pltpu.CompilerParams(vmem_limit_bytes=48 * 1024 * 1024)


def f32(*shape):
    return jax.ShapeDtypeStruct(shape, jnp.float32)


def smoothing(block):
    second = np.zeros((block - 2, block), np.float32)
    for row in range(block - 2):
        second[row, row : row + 3] = (1.0, -2.0, 1.0)
    return second.T @ second


def cols_dot(left, right):
    return lax.dot_general(
        left, right, (((0,), (0,)), ((), ())), precision=HIGHEST,
        preferred_element_type=jnp.float32,
    )


def lanes_dot(left, right):
    return lax.dot_general(
        left, right, (((1,), (1,)), ((), ())), precision=HIGHEST,
        preferred_element_type=jnp.float32,
    )


def grid_iota():
    sub = lax.broadcasted_iota(jnp.int32, (SUB, LANES), 0)
    lane = lax.broadcasted_iota(jnp.int32, (SUB, LANES), 1)
    return sub, lane


def first_knot(group, plane, knots):
    return lax.div(group * (GROUP * (knots - 3)), plane)


def clear(ref):
    ref[...] = jnp.zeros(ref.shape, ref.dtype)


def to_planes(depth, groups, flat_ref, out_ref):
    rows = groups * SUB
    for z in range(depth):
        out_ref[z, 0:FRONT, :] = jnp.zeros((FRONT, LANES), jnp.float32)
        out_ref[z, FRONT + rows : FRONT + rows + BACK, :] = jnp.zeros((BACK, LANES), jnp.float32)

    def body(group, _):
        for z in range(depth):
            out_ref[z, pl.ds(pl.multiple_of(FRONT + group * SUB, SUB), SUB), :] = flat_ref[
                pl.ds(group * (SUB * depth) + z, SUB, stride=depth), :
            ]
        return 0

    lax.fori_loop(0, groups, body, 0)


def lane_sums(acc, knots):
    partial = jnp.sum(acc[0:knots], axis=1)
    return lanes_dot(jnp.ones((SUB, LANES), jnp.float32), partial)[0:1, :]


def own_kernel(
    depth, plane, knots, table, image, slope, basis, weight, pull, bands, image_planes,
    slope_planes, count, acc,
):
    groups = plane // GROUP
    sub, lane = grid_iota()
    place0 = sub * LANES + lane
    to_planes(depth, groups, image, image_planes)
    to_planes(depth, groups, slope, slope_planes)
    clear(count)
    clear(acc)

    def add_pair(pair, _):
        off = table[pair, 3]
        live = table[pair, 4].astype(jnp.float32)
        row = lax.shift_right_logical(off, 10) * SUB
        low = off & (GROUP - 1)
        for i in range(SPAN):
            at = pl.ds(pl.multiple_of(FRONT + row + i * SUB, SUB), SUB)
            s = place0 + (i * GROUP - low)
            count[at, :] += jnp.where((s >= 0) & (s < SLAB), live, 0.0)
        return 0

    lax.fori_loop(0, table.shape[0], add_pair, 0)

    def body(group, _):
        at = pl.ds(pl.multiple_of(FRONT + group * SUB, SUB), SUB)
        squares = jnp.zeros((SUB, LANES), jnp.float32)
        cross = jnp.zeros((SUB, LANES), jnp.float32)
        for z in range(depth):
            g = slope_planes[z, at, :]
            squares += g * g
            cross += g * image_planes[z, at, :]
        w = squares * count[at, :]
        here = pl.ds(pl.multiple_of(group * SUB, SUB), SUB)
        weight[here, :] = w
        pull[here, :] = cross * count[at, :]
        first = first_knot(group, plane, knots)
        place = (place0 + group * GROUP).astype(jnp.float32) * ((knots - 3) / plane) + 1.0
        parts = []
        for i in range(WINDOW):
            dist = jnp.abs(place - (first + i).astype(jnp.float32))
            inner = 2.0 / 3.0 - dist * dist + 0.5 * dist * dist * dist
            outer = (2.0 - dist) * (2.0 - dist) * (2.0 - dist) * (1.0 / 6.0)
            value = jnp.where(dist < 1.0, inner, jnp.where(dist < 2.0, outer, 0.0))
            basis[group * WINDOW + i] = value
            parts.append(value)
        for i in range(WINDOW):
            scaled = parts[i] * w
            for d in range(min(BAND, WINDOW - i)):
                acc[d, first + i] += scaled * parts[i + d]
        return 0

    lax.fori_loop(0, groups, body, 0)
    bands[...] = jnp.concatenate(
        [lane_sums(acc.at[d], knots) for d in range(BAND)]
        + [jnp.zeros((SUB - BAND, LANES), jnp.float32)],
        axis=0,
    )


def pair_place(table, pair):
    low = table[pair, 1] & (GROUP - 1)
    start = table[pair, 1] - low
    shift = table[pair, 3] - low
    row_b = pl.multiple_of(FRONT + lax.shift_right_logical(start, 7), SUB)
    row_a = FRONT + lax.shift_right_arithmetic(shift, 7)
    return low, row_b, row_a, shift & (LANES - 1)


def pair_kernel(depth, plane, table, far_slope, image_planes, slope_planes, image_sum, slope_sum, far):
    sub, lane = grid_iota()
    place0 = sub * LANES + lane
    to_planes(depth, plane // GROUP, far_slope, far)

    def body(pair, _):
        low, row_b, row_a, turn = pair_place(table, pair)
        live = table[pair, 4].astype(jnp.float32)
        back = (LANES - turn) & (LANES - 1)
        keep = lane >= turn
        for i in range(SPAN):
            at = pl.ds(pl.multiple_of(row_b + i * SUB, SUB), SUB)
            c = jnp.zeros((SUB, LANES), jnp.float32)
            d = jnp.zeros((SUB, LANES), jnp.float32)
            for z in range(depth):
                a = jnp.where(
                    keep,
                    far[z, pl.ds(row_a + i * SUB, SUB), :],
                    far[z, pl.ds(row_a + i * SUB + 1, SUB), :],
                )
                a = pltpu.roll(a, back, 1)
                c += a * image_planes[z, at, :]
                d += a * slope_planes[z, at, :]
            s = place0 + (i * GROUP - low)
            inside = (s >= 0) & (s < SLAB)
            image_sum[pair, pl.ds(i * SUB, SUB), :] = jnp.where(inside, c * live, 0.0)
            slope_sum[pair, pl.ds(i * SUB, SUB), :] = jnp.where(inside, d * live, 0.0)
        return 0

    lax.fori_loop(0, table.shape[0], body, 0)


def project_kernel(
    plane, knots, cap, table, coef, rigid, basis, weight, pull, c0, d0, c1, d1, c2, d2,
    grads, field, landed, acc,
):
    groups = plane // GROUP
    rows = plane // LANES
    sub, lane = grid_iota()
    field[0:FRONT, :] = jnp.zeros((FRONT, LANES), jnp.float32)
    field[FRONT + rows : FRONT + rows + BACK, :] = jnp.zeros((BACK, LANES), jnp.float32)
    clear(landed)
    clear(acc)
    base = shift_step * rigid[0].astype(jnp.float32)

    def fill(group, _):
        first = first_knot(group, plane, knots)
        value = jnp.zeros((SUB, LANES), jnp.float32)
        for i in range(WINDOW):
            value += coef[first + i] * basis[group * WINDOW + i]
        field[pl.ds(pl.multiple_of(FRONT + group * SUB, SUB), SUB), :] = value + base
        return 0

    lax.fori_loop(0, groups, fill, 0)

    for side, (c, d) in enumerate(((c0, d0), (c1, d1), (c2, d2))):

        def body(pair, _):
            low, row_b, row_a, turn = pair_place(table, side * cap + pair)
            keep = lane >= turn
            for i in range(SPAN):
                at = pl.ds(pl.multiple_of(row_b + i * SUB, SUB), SUB)
                here = pl.ds(i * SUB, SUB)
                term = c[pair, here, :] + field[at, :] * d[pair, here, :]
                term = pltpu.roll(term, turn, 1)
                landed[side, pl.ds(row_a + i * SUB, SUB), :] += jnp.where(keep, term, 0.0)
                landed[side, pl.ds(row_a + i * SUB + 1, SUB), :] += jnp.where(keep, 0.0, term)
            return 0

        lax.fori_loop(0, cap, body, 0)

    def gather(group, _):
        first = first_knot(group, plane, knots)
        at = pl.ds(pl.multiple_of(FRONT + group * SUB, SUB), SUB)
        here = pl.ds(pl.multiple_of(group * SUB, SUB), SUB)
        own = pull[here, :] + weight[here, :] * field[at, :] - landed[1, at, :]
        values = (own, -landed[0, at, :], -landed[2, at, :])
        for i in range(WINDOW):
            b = basis[group * WINDOW + i]
            for q in range(3):
                acc[q, first + i] += b * values[q]
        return 0

    lax.fori_loop(0, groups, gather, 0)
    grads[...] = jnp.concatenate(
        [lane_sums(acc.at[q], knots) for q in range(3)]
        + [jnp.zeros((SUB - 3, LANES), jnp.float32)],
        axis=0,
    )


def share_kernel(knot_count, total, mine, out, held, send_sem, recv_sem):
    me = lax.axis_index("tile") * knot_count + lax.axis_index("knot")

    def peer(step):
        other = lax.rem(me + step, total)
        return other, (lax.div(other, knot_count), lax.rem(other, knot_count))

    barrier = pltpu.get_barrier_semaphore()

    def greet(step, _):
        pl.semaphore_signal(barrier, inc=1, device_id=peer(step)[1], device_id_type=MESH)
        return 0

    lax.fori_loop(1, total, greet, 0)
    pl.semaphore_wait(barrier, total - 1)

    def copy(step, slot):
        return pltpu.make_async_remote_copy(
            src_ref=mine,
            dst_ref=held.at[slot],
            send_sem=send_sem.at[step],
            recv_sem=recv_sem.at[slot],
            device_id=peer(step)[1],
            device_id_type=MESH,
        )

    def send(step, _):
        copy(step, me).start()
        return 0

    lax.fori_loop(1, total, send, 0)
    held[me] = mine[...]

    def arrive(step, _):
        copy(step, peer(step)[0]).wait_recv()
        return 0

    lax.fori_loop(1, total, arrive, 0)
    out[...] = held[...]

    def sent(step, _):
        copy(step, me).wait_send()
        return 0

    lax.fori_loop(1, total, sent, 0)


def local_rows(index, coef):
    sub = lax.broadcasted_iota(jnp.int32, (SUB, LANES), 0)
    lane = lax.broadcasted_iota(jnp.int32, (SUB, LANES), 1)
    want = jnp.where(sub == 0, index[0], jnp.where(sub == 1, index[1], index[2]))
    hot = ((lane == want) & (sub < 3)).astype(jnp.float32)
    return lanes_dot(hot, coef)


def halves(value, block):
    return jnp.concatenate([value[:, 0:block], value[:, block : 2 * block]], axis=0)


def factor_kernel(tile_count, knot_count, block, index, shared, factors, chosen, coef, local, system):
    total = tile_count * knot_count
    bands = jnp.sum(shared[...].reshape(tile_count, knot_count, SUB, LANES), axis=1)
    labels = shared[...].reshape(tile_count, knot_count, SUB, LANES)[:, 0, BAND, :]
    labels = jnp.concatenate([labels[:, 0:1], labels[:, 1:2]], axis=0)
    lane = lax.broadcasted_iota(jnp.int32, (2 * tile_count, LANES), 1).astype(jnp.float32)
    select = (lane == labels).astype(jnp.float32)
    chosen[...] = select
    row = lax.broadcasted_iota(jnp.int32, (total, LANES), 0)
    col = lax.broadcasted_iota(jnp.int32, (total, LANES), 1)
    start = cols_dot(shared[:, BAND + 1, 0:block], (row == col).astype(jnp.float32))
    coef[...] = start
    local[...] = local_rows(index, start)
    for d in range(BAND):
        system[d] = cols_dot(halves(bands[:, d, :], block), select)
    penalty = smoothing(block)

    def entry(k, d):
        extra = smooth_weight * float(penalty[k - d, k]) + (ridge_weight if d == 0 else 0.0)
        return jnp.broadcast_to(system[d, k - d : k - d + 1, :], (SUB, LANES)) + extra

    zero = jnp.zeros((SUB, LANES), jnp.float32)
    rows = []
    for k in range(block):
        p1, q1, r1, i1 = rows[k - 1] if k >= 1 else (zero,) * 4
        p2, q2, r2, i2 = rows[k - 2] if k >= 2 else (zero,) * 4
        p3, q3, r3, i3 = rows[k - 3] if k >= 3 else (zero,) * 4
        ur = entry(k, 3) if k >= 3 else zero
        uq = entry(k, 2) - ur * p2 if k >= 2 else zero
        up = entry(k, 1) - ur * q1 - uq * p1 if k >= 1 else zero
        r, q, p = ur * i3, uq * i2, up * i1
        inverse = 1.0 / (entry(k, 0) - ur * r - uq * q - up * p)
        rows.append((p, q, r, inverse))
        for which, value in enumerate((p, q, r, inverse)):
            factors[which, k] = value


def solve_kernel(
    tile_count, knot_count, block, index, shared, chosen, factors, coef, penalty,
    coef_out, local, work,
):
    sums = jnp.sum(shared[...].reshape(tile_count, knot_count, SUB, LANES), axis=1)
    own, lower, upper = sums[:, 0, :], sums[:, 1, :], sums[:, 2, :]
    none = jnp.zeros((1, LANES), jnp.float32)
    grads = (
        own
        + jnp.concatenate([lower[1:, :], none], axis=0)
        + jnp.concatenate([none, upper[:-1, :]], axis=0)
    )
    grad_sum = cols_dot(halves(grads, block), chosen[...])
    bend = jnp.dot(
        penalty[...], coef[...], precision=HIGHEST, preferred_element_type=jnp.float32
    )
    work[...] = -(grad_sum + smooth_weight * bend)
    forward = []
    for k in range(block):
        value = jnp.broadcast_to(work[k : k + 1, :], (SUB, LANES))
        for back in (3, 2, 1):
            if k >= back:
                value = value - factors[back - 1, k] * forward[k - back]
        forward.append(value)
    steps = [None] * block
    for k in reversed(range(block)):
        value = forward[k] * factors[3, k]
        for ahead in (3, 2, 1):
            if k + ahead < block:
                value = value - factors[ahead - 1, k + ahead] * steps[k + ahead]
        steps[k] = value
        work[k : k + 1, :] = value[0:1, :]
    fresh = coef[...] + work[...]
    coef_out[...] = fresh
    local[...] = local_rows(index, fresh)


def warp_kernel(plane, knots, depth, coef, rigid, basis, image, slope, out):
    step = pl.program_id(0)
    base = shift_step * rigid[0].astype(jnp.float32)
    count = basis.shape[0] // WINDOW

    def body(at, _):
        group = step * count + at
        first = first_knot(group, plane, knots)
        value = jnp.zeros((SUB, LANES), jnp.float32)
        for i in range(WINDOW):
            value += coef[first + i] * basis[at * WINDOW + i]
        value += base
        for r in range(SUB):
            here = pl.ds(pl.multiple_of((at * SUB + r) * depth, depth), depth)
            out[here, :] = image[here, :] + slope[here, :] * value[r : r + 1, :]
        return 0

    lax.fori_loop(0, count, body, 0)


def per_device(images, gradient, shifts, tile_blocks, intersections, start_coefficients):
    depth, plane = images.shape[1:]
    block = start_coefficients.shape[1]
    knots = 2 * block
    groups = plane // GROUP
    rows = plane // LANES
    padded = FRONT + rows + BACK
    tile_count = lax.axis_size("tile")
    knot_count = lax.axis_size("knot")
    total = tile_count * knot_count
    cap = intersections.shape[2]
    me = lax.axis_index("tile") * knot_count + lax.axis_index("knot")
    links = intersections[0]
    table = links.reshape(3 * cap, 5)

    def flat(volume):
        volume = volume.reshape(depth, rows, LANES).transpose(1, 0, 2)
        return volume.reshape(rows * depth, LANES)

    def route(value, distance):
        pairs = [
            (i - distance, i) for i in range(tile_count) if 0 <= i - distance < tile_count
        ]
        return lax.ppermute(value, "tile", pairs)

    image, slope = flat(images[0]), flat(gradient[0])
    incoming = jnp.concatenate([route(links[2], 1), links[1], route(links[0], -1)], axis=0)
    slope_below, slope_above = flat(route(gradient, 1)[0]), flat(route(gradient, -1)[0])

    basis, weight, pull, bands, image_planes, slope_planes = pl.pallas_call(
        functools.partial(own_kernel, depth, plane, knots),
        out_shape=(
            f32(groups * WINDOW, SUB, LANES),
            f32(rows, LANES),
            f32(rows, LANES),
            f32(SUB, LANES),
            f32(depth, padded, LANES),
            f32(depth, padded, LANES),
        ),
        in_specs=[SMEM, VMEM, VMEM],
        out_specs=(VMEM,) * 6,
        scratch_shapes=[
            pltpu.VMEM((padded, LANES), jnp.float32),
            pltpu.VMEM((BAND, knots + 8, SUB, LANES), jnp.float32),
        ],
        compiler_params=PARAMS,
        cost_estimate=pl.CostEstimate(
            flops=100 * plane, bytes_accessed=12 * depth * plane, transcendentals=0
        ),
        name="own",
    )(incoming, image, slope)

    def share(value):
        return pl.pallas_call(
            functools.partial(share_kernel, knot_count, total),
            out_shape=f32(total, SUB, LANES),
            in_specs=[VMEM],
            out_specs=VMEM,
            scratch_shapes=[
                pltpu.VMEM((total, SUB, LANES), jnp.float32),
                pltpu.SemaphoreType.DMA((total,)),
                pltpu.SemaphoreType.DMA((total,)),
            ],
            compiler_params=pltpu.CompilerParams(collective_id=0, has_side_effects=True),
            name="share",
        )(value)

    def pairs(which, far):
        return pl.pallas_call(
            functools.partial(pair_kernel, depth, plane),
            out_shape=(f32(cap, SPAN * SUB, LANES),) * 2,
            in_specs=[SMEM] + [VMEM] * 3,
            out_specs=(VMEM,) * 2,
            scratch_shapes=[pltpu.VMEM((depth, padded, LANES), jnp.float32)],
            compiler_params=PARAMS,
            cost_estimate=pl.CostEstimate(
                flops=4 * depth * cap * SLAB,
                bytes_accessed=12 * depth * plane,
                transcendentals=0,
            ),
            name="pairs",
        )(links[which], far, image_planes, slope_planes)

    facts = jnp.concatenate(
        [
            bands[0:BAND],
            jnp.pad(tile_blocks.astype(jnp.float32), ((0, 0), (0, LANES - 2))),
            jnp.pad(start_coefficients, ((0, 0), (0, LANES - block))),
            bands[BAND + 2 :],
        ],
        axis=0,
    )
    index = jnp.concatenate([tile_blocks[0], me[None].astype(jnp.int32)])
    factors, chosen, coef, local = pl.pallas_call(
        functools.partial(factor_kernel, tile_count, knot_count, block),
        out_shape=(
            f32(4, block, SUB, LANES),
            f32(2 * tile_count, LANES),
            f32(block, LANES),
            f32(SUB, block),
        ),
        in_specs=[SMEM, VMEM],
        out_specs=(VMEM,) * 4,
        scratch_shapes=[pltpu.VMEM((BAND, block, LANES), jnp.float32)],
        compiler_params=PARAMS,
        name="factor",
    )(index, share(facts))
    sums = pairs(1, slope)
    sums = (*pairs(0, slope_below), *sums, *pairs(2, slope_above))
    penalty = jnp.asarray(smoothing(block))

    def scalars(rows_of):
        return jnp.pad(rows_of[0:2].reshape(knots), (0, 8))

    for step in range(ITERS):
        grads = pl.pallas_call(
            functools.partial(project_kernel, plane, knots, cap),
            out_shape=f32(SUB, LANES),
            in_specs=[SMEM] * 3 + [VMEM] * 9,
            out_specs=VMEM,
            scratch_shapes=[
                pltpu.VMEM((padded, LANES), jnp.float32),
                pltpu.VMEM((3, padded, LANES), jnp.float32),
                pltpu.VMEM((3, knots + 8, SUB, LANES), jnp.float32),
            ],
            compiler_params=PARAMS,
            name="project",
        )(table, scalars(local), shifts, basis, weight, pull, *sums)
        coef, local = pl.pallas_call(
            functools.partial(solve_kernel, tile_count, knot_count, block),
            out_shape=(f32(block, LANES), f32(SUB, block)),
            in_specs=[SMEM] + [VMEM] * 5,
            out_specs=(VMEM,) * 2,
            scratch_shapes=[pltpu.VMEM((block, LANES), jnp.float32)],
            compiler_params=PARAMS,
            name="solve",
        )(index, share(grads), chosen, factors, coef, penalty)

    cuts = 8
    part = pl.BlockSpec((rows * depth // cuts, LANES), lambda i: (i, 0))
    warped = pl.pallas_call(
        functools.partial(warp_kernel, plane, knots, depth),
        out_shape=f32(rows * depth, LANES),
        grid=(cuts,),
        in_specs=[
            SMEM,
            SMEM,
            pl.BlockSpec((groups * WINDOW // cuts, SUB, LANES), lambda i: (i, 0, 0)),
            part,
            part,
        ],
        out_specs=part,
        compiler_params=PARAMS,
        name="warp",
    )(scalars(local), shifts, basis, image, slope)
    warped = warped.reshape(rows, depth, LANES).transpose(1, 0, 2).reshape(1, depth, plane)
    return local[2:3], warped


def solution(mesh):
    placed = (
        P("tile", "knot", None),
        P("tile", "knot", None),
        P("tile"),
        P("tile", None),
        P("tile", None, None, None),
        P(("tile", "knot"), None),
    )
    return jax.shard_map(
        per_device,
        mesh=mesh,
        in_specs=placed,
        out_specs=(P(("tile", "knot"), None), P("tile", "knot", None)),
        check_vma=False,
    )
```

```python
import functools
import math

import jax
import jax.numpy as jnp
import numpy as np
from jax import lax
from jax.experimental import pallas as pl
from jax.experimental.pallas import tpu as pltpu
from jax.sharding import PartitionSpec as P

SLAB = 8192
ITERS = 2
LANES = 128
SUB = 8
GROUP = SUB * LANES
FRONT = 8
BACK = 16
WINDOW = 6
BAND = 4
CHUNKS = 4
SPAN = SLAB // GROUP + 1

shift_step = 0.05
smooth_weight = 20.0
ridge_weight = 1.0
HIGHEST = lax.Precision.HIGHEST
MESH = pl.DeviceIdType.MESH
VMEM = pl.BlockSpec(memory_space=pltpu.VMEM)
SMEM = pl.BlockSpec(memory_space=pltpu.SMEM)
ANY = pl.BlockSpec(memory_space=pl.ANY)
PARAMS = pltpu.CompilerParams(vmem_limit_bytes=16 * 1024 * 1024)


def f32(*shape):
    return jax.ShapeDtypeStruct(shape, jnp.float32)


def smoothing(block):
    second = np.zeros((block - 2, block), np.float32)
    for row in range(block - 2):
        second[row, row : row + 3] = (1.0, -2.0, 1.0)
    return second.T @ second


def cols_dot(left, right):
    return lax.dot_general(
        left, right, (((0,), (0,)), ((), ())), precision=HIGHEST,
        preferred_element_type=jnp.float32,
    )


def lanes_dot(left, right):
    return lax.dot_general(
        left, right, (((1,), (1,)), ((), ())), precision=HIGHEST,
        preferred_element_type=jnp.float32,
    )


def grid_iota():
    sub = lax.broadcasted_iota(jnp.int32, (SUB, LANES), 0)
    lane = lax.broadcasted_iota(jnp.int32, (SUB, LANES), 1)
    return sub, lane


def first_knot(group, plane, knots):
    return lax.div(group * (GROUP * (knots - 3)), plane)


def clear(ref):
    ref[...] = jnp.zeros(ref.shape, ref.dtype)


def lane_sums(partial):
    return lanes_dot(jnp.ones((SUB, LANES), jnp.float32), jnp.sum(partial, axis=1))[0:1, :]


def row_sums(values):
    sub = lax.broadcasted_iota(jnp.int32, (SUB, LANES), 0)
    for bit in (1, 2, 4):
        low = (sub & bit) == 0
        values = [
            jnp.where(low, a, b) + pltpu.roll(jnp.where(low, b, a), bit, 0)
            for a, b in zip(values[0::2], values[1::2])
        ]
    return values[0]


def spread(ref, row):
    return jnp.broadcast_to(ref[row : row + 1, :], (SUB, LANES))


def greet(tile_count, knot_count):
    tile, knot = lax.axis_index("tile"), lax.axis_index("knot")
    barrier = pltpu.get_barrier_semaphore()
    for step in range(1, knot_count):
        pl.semaphore_signal(
            barrier, inc=1, device_id=(tile, lax.rem(knot + step, knot_count)), device_id_type=MESH
        )

    def call(step, _):
        pl.semaphore_signal(
            barrier, inc=1, device_id=(lax.rem(tile + step, tile_count), knot), device_id_type=MESH
        )
        return 0

    lax.fori_loop(1, tile_count, call, 0)
    pl.semaphore_wait(barrier, tile_count + knot_count - 2)


def share_scratch(tile_count, knot_count, rows):
    return [
        pltpu.VMEM((rows, LANES), jnp.float32),
        pltpu.VMEM((knot_count, rows, LANES), jnp.float32),
        pltpu.VMEM((tile_count, rows, LANES), jnp.float32),
        pltpu.SemaphoreType.DMA((knot_count,)),
        pltpu.SemaphoreType.DMA((knot_count,)),
        pltpu.SemaphoreType.DMA((tile_count,)),
        pltpu.SemaphoreType.DMA((tile_count,)),
    ]


def share(tile_count, knot_count, mine, scratch, between=None):
    total, column, table, send_a, recv_a, send_b, recv_b = scratch
    tile, knot = lax.axis_index("tile"), lax.axis_index("knot")

    def over_knot(step, slot):
        return pltpu.make_async_remote_copy(
            src_ref=mine,
            dst_ref=column.at[slot],
            send_sem=send_a.at[step],
            recv_sem=recv_a.at[slot],
            device_id=(tile, lax.rem(knot + step, knot_count)),
            device_id_type=MESH,
        )

    def over_tile(step, slot):
        return pltpu.make_async_remote_copy(
            src_ref=total,
            dst_ref=table.at[slot],
            send_sem=send_b.at[step],
            recv_sem=recv_b.at[slot],
            device_id=(lax.rem(tile + step, tile_count), knot),
            device_id_type=MESH,
        )

    for step in range(1, knot_count):
        over_knot(step, knot).start()
    column[knot] = mine[...]
    if between is not None:
        between(0)
    for step in range(1, knot_count):
        over_knot(step, lax.rem(knot + step, knot_count)).wait_recv()
    total[...] = jnp.sum(column[...], axis=0)

    def send(step, _):
        over_tile(step, tile).start()
        return 0

    lax.fori_loop(1, tile_count, send, 0)
    table[tile] = total[...]
    if between is not None:
        between(1)

    def arrive(step, _):
        over_tile(step, lax.rem(tile + step, tile_count)).wait_recv()
        return 0

    lax.fori_loop(1, tile_count, arrive, 0)

    def finish():
        for step in range(1, knot_count):
            over_knot(step, knot).wait_send()

        def sent(step, _):
            over_tile(step, tile).wait_send()
            return 0

        lax.fori_loop(1, tile_count, sent, 0)

    return table, finish


def halves(value, block):
    return jnp.concatenate([value[:, 0:block], value[:, block : 2 * block]], axis=0)


def spread_coef(blocks, coef, out):
    block = coef.shape[0]
    sub = lax.broadcasted_iota(jnp.int32, (LANES, LANES), 0)
    for n in range(2):
        hot = (sub == blocks[0, n]).astype(jnp.float32)
        out[n * block : (n + 1) * block, :] = jnp.dot(
            coef, hot, precision=HIGHEST, preferred_element_type=jnp.float32
        )
    out[2 * block : 2 * block + SUB, :] = jnp.zeros((SUB, LANES), jnp.float32)


def factor(block, penalty, system, factors):
    def entry(k, d):
        extra = smooth_weight * float(penalty[k - d, k]) + (ridge_weight if d == 0 else 0.0)
        return spread(system.at[d], k - d) + extra

    zero = jnp.zeros((SUB, LANES), jnp.float32)
    rows = []
    for k in range(block):
        p1, q1, r1, i1 = rows[k - 1] if k >= 1 else (zero,) * 4
        p2, q2, r2, i2 = rows[k - 2] if k >= 2 else (zero,) * 4
        p3, q3, r3, i3 = rows[k - 3] if k >= 3 else (zero,) * 4
        ur = entry(k, 3) if k >= 3 else zero
        uq = entry(k, 2) - ur * p2 if k >= 2 else zero
        up = entry(k, 1) - ur * q1 - uq * p1 if k >= 1 else zero
        r, q, p = ur * i3, uq * i2, up * i1
        inverse = 1.0 / (entry(k, 0) - ur * r - uq * q - up * p)
        rows.append((p, q, r, inverse))
        for which, value in enumerate((p, q, r, inverse)):
            factors[which, k] = value


def pair_place(table, side, pair):
    low = table[0, side, pair, 1] & (GROUP - 1)
    start = table[0, side, pair, 1] - low
    shift = table[0, side, pair, 3] - low
    row_b = pl.multiple_of(FRONT + lax.shift_right_logical(start, 7), SUB)
    row_a = FRONT + lax.shift_right_arithmetic(shift, 7)
    return low, row_b, row_a, shift & (LANES - 1)


def pair_sums(table, side, cap, far, image, slope, image_sum, slope_sum):
    sub, lane = grid_iota()
    place0 = sub * LANES + lane

    def body(at, _):
        pair = side * cap + at
        low, row_b, row_a, turn = pair_place(table, side, at)
        live = table[0, side, at, 4].astype(jnp.float32)
        back = (LANES - turn) & (LANES - 1)
        keep = lane >= turn
        for i in range(SPAN):
            c, d = [], []
            for r in range(SUB):
                row = i * SUB + r
                a = jnp.where(keep, far[row_a + row], far[row_a + (row + 1)])
                a = pltpu.roll(a, back, 1)
                c.append(a * image[row_b + row])
                d.append(a * slope[row_b + row])
            s = place0 + (i * GROUP - low)
            inside = (s >= 0) & (s < SLAB) & (live != 0.0)
            image_sum[pair, pl.ds(i * SUB, SUB), :] = jnp.where(inside, row_sums(c) * live, 0.0)
            slope_sum[pair, pl.ds(i * SUB, SUB), :] = jnp.where(inside, row_sums(d) * live, 0.0)
        return 0

    lax.fori_loop(0, cap, body, 0)


def pair_kernel(
    rows, cap, table, image, slope, below, above, image_sum, slope_sum,
    own_image, own_slope, own_below, own_above, sem,
):
    middle = pl.ds(FRONT, rows)
    loads = [
        pltpu.make_async_copy(src, dst.at[middle], sem.at[i])
        for i, (src, dst) in enumerate(
            ((image, own_image), (slope, own_slope), (below, own_below), (above, own_above))
        )
    ]
    for load in loads:
        load.start()
    loads[0].wait()
    loads[1].wait()
    pair_sums(table, 1, cap, own_slope, own_image, own_slope, image_sum, slope_sum)
    loads[2].wait()
    pair_sums(table, 0, cap, own_below, own_image, own_slope, image_sum, slope_sum)
    loads[3].wait()
    pair_sums(table, 2, cap, own_above, own_image, own_slope, image_sum, slope_sum)


def begin_kernel(
    depth, plane, block, tile_count, knot_count, cap, wide,
    blocks, table, first_coef, image, slope,
    basis, weight, pull, below, above, factors, chosen, coef, local,
    own_image, own_slope, passing, tabs, tabs_in, acc, system, mine,
    here_sem, tab_send, tab_recv, big_send, big_recv, chunk_send, chunk_recv, pass_send, pass_recv,
    *share_refs,
):
    knots = 2 * block
    rows = plane // LANES
    groups = plane // GROUP
    half, piece = rows // 2, rows // 2 // CHUNKS
    tile, knot = lax.axis_index("tile"), lax.axis_index("knot")
    pos = lax.rem(tile, wide) if wide else tile
    sub, lane = grid_iota()
    place0 = sub * LANES + lane
    land = (below, above)
    loads = [
        pltpu.make_async_copy(image, own_image, here_sem.at[0]),
        pltpu.make_async_copy(slope, own_slope, here_sem.at[1]),
    ]
    for load in loads:
        load.start()
    for d in range(3):
        for m in range(cap):
            for row, part in ((m, 3), (cap + m, 4)):
                value = table[0, d, m, part].astype(jnp.float32)
                tabs[d, row : row + 1, :] = jnp.full((1, LANES), value)
    greet(tile_count, knot_count)

    def remote(src, dst, send_sem, recv_sem, to):
        return pltpu.make_async_remote_copy(
            src_ref=src, dst_ref=dst, send_sem=send_sem, recv_sem=recv_sem,
            device_id=(to, knot), device_id_type=MESH,
        )

    def tab_copy(side):
        return remote(
            tabs.at[2 - 2 * side], tabs_in.at[side], tab_send.at[side], tab_recv.at[side],
            tile + (1 - 2 * side),
        )

    def direct(side, count):
        return remote(
            slope.at[pl.ds(0, count)], land[side].at[pl.ds(0, count)],
            big_send.at[side], big_recv.at[side], tile + (1 - 2 * side),
        )

    def to_relay(side, c):
        return remote(
            slope.at[pl.ds(half + c * piece, piece)], passing.at[pl.ds(c * piece, piece)],
            chunk_send.at[c], chunk_recv.at[c], tile + (wide - 2 * wide * side),
        )

    def from_relay(side, c):
        return remote(
            passing.at[pl.ds(c * piece, piece)],
            land[side].at[pl.ds(half + c * piece, piece)],
            pass_send.at[c], pass_recv.at[c], tile + (1 - wide if side == 0 else wide - 1),
        )

    goes = (tile + 1 < tile_count, tile > 0)
    comes = (tile > 0, tile + 1 < tile_count)
    if wide:
        edge_out = (pos == wide - 1, pos == 0)
        edge_in = (pos == 0, pos == wide - 1)
        relays = ((pos == wide - 1) & (tile >= wide), (pos == 0) & (tile + wide < tile_count))

    def when(*terms):
        flag = terms[0]
        for term in terms[1:]:
            flag = flag & term
        return pl.when(flag)

    for side in range(2):
        when(goes[side])(lambda side=side: tab_copy(side).start())
    for side in range(2):
        if wide:
            def split(side=side):
                for c in range(CHUNKS):
                    to_relay(side, c).start()
                direct(side, half).start()

            when(goes[side], edge_out[side])(split)
            when(goes[side], jnp.logical_not(edge_out[side]))(
                lambda side=side: direct(side, rows).start()
            )
        else:
            when(goes[side])(lambda side=side: direct(side, rows).start())

    def forward(c):
        if wide:
            for side in range(2):
                def hand_on(side=side):
                    to_relay(side, c).wait_recv()
                    from_relay(side, c).start()

                when(relays[side])(hand_on)

    clear(acc)
    for load in loads:
        load.wait()

    def squares(group, _):
        gg, gi = [], []
        for r in range(SUB):
            row = group * SUB + r
            g = own_slope[row]
            gg.append(g * g)
            gi.append(g * own_image[row])
        here = pl.ds(pl.multiple_of(group * SUB, SUB), SUB)
        weight[here, :] = row_sums(gg)
        pull[here, :] = row_sums(gi)
        return 0

    lax.fori_loop(0, groups, squares, 0)
    forward(0)
    for side in range(2):
        when(comes[side])(lambda side=side: tab_copy(side).wait_recv())

        def absent(side=side):
            tabs_in[side] = jnp.zeros((2 * cap, LANES), jnp.float32)

        when(jnp.logical_not(comes[side]))(absent)

    def body(group, _):
        here = pl.ds(pl.multiple_of(group * SUB, SUB), SUB)
        at = (place0 + group * GROUP).astype(jnp.float32)
        count = jnp.zeros((SUB, LANES), jnp.float32)
        for source in (tabs_in.at[0], tabs.at[1], tabs_in.at[1]):
            for m in range(cap):
                s = at - spread(source, m)
                inside = (s >= 0.0) & (s < float(SLAB))
                count += jnp.where(inside, spread(source, cap + m), 0.0)
        w = weight[here, :] * count
        weight[here, :] = w
        pull[here, :] = pull[here, :] * count
        first = first_knot(group, plane, knots)
        place = at * ((knots - 3) / plane) + 1.0
        parts = []
        for i in range(WINDOW):
            dist = jnp.abs(place - (first + i).astype(jnp.float32))
            inner = 2.0 / 3.0 - dist * dist + 0.5 * dist * dist * dist
            outer = (2.0 - dist) * (2.0 - dist) * (2.0 - dist) * (1.0 / 6.0)
            value = jnp.where(dist < 1.0, inner, jnp.where(dist < 2.0, outer, 0.0))
            basis[group * WINDOW + i] = value
            parts.append(value)
        for i in range(WINDOW):
            scaled = parts[i] * w
            for d in range(min(BAND, WINDOW - i)):
                acc[d, first + i] += scaled * parts[i + d]
        return 0

    lax.fori_loop(0, groups, body, 0)
    forward(1)
    clear(mine)
    for d in range(BAND):
        mine[d : d + 1, :] = lane_sums(acc[d, 0:knots])
    lane_row = lax.broadcasted_iota(jnp.int32, (1, LANES), 1)
    label = jnp.where(
        lane_row == 0,
        blocks[0, 0].astype(jnp.float32),
        jnp.where(lane_row == 1, blocks[0, 1].astype(jnp.float32), 0.0),
    )
    mine[BAND : BAND + 1, :] = jnp.where(knot == 0, label, 0.0)
    mine[pl.ds(SUB + knot, 1), 0:block] = first_coef[...]
    shared, finish = share(
        tile_count, knot_count, mine, share_refs, lambda stage: forward(2 + stage)
    )
    bands = shared[...]
    labels = bands[:, BAND, :]
    labels = jnp.concatenate([labels[:, 0:1], labels[:, 1:2]], axis=0)
    wide_lane = lax.broadcasted_iota(jnp.int32, (2 * tile_count, LANES), 1).astype(jnp.float32)
    select = (wide_lane == labels).astype(jnp.float32)
    chosen[...] = select
    row = lax.broadcasted_iota(jnp.int32, (tile_count, LANES), 0) * knot_count
    col = lax.broadcasted_iota(jnp.int32, (tile_count, LANES), 1)
    start = jnp.zeros((block, LANES), jnp.float32)
    for k in range(knot_count):
        start += cols_dot(bands[:, SUB + k, 0:block], (row + k == col).astype(jnp.float32))
    coef[...] = start
    spread_coef(blocks, start, local)
    for d in range(BAND):
        system[d] = cols_dot(halves(bands[:, d, :], block), select)
    factor(block, smoothing(block), system, factors)

    for side in range(2):
        if wide:
            def pieces(side=side):
                direct(side, half).wait_recv()
                for c in range(CHUNKS):
                    from_relay(side, c).wait_recv()

            when(comes[side], edge_in[side])(pieces)
            when(comes[side], jnp.logical_not(edge_in[side]))(
                lambda side=side: direct(side, rows).wait_recv()
            )
        else:
            when(comes[side])(lambda side=side: direct(side, rows).wait_recv())
    finish()
    for side in range(2):
        when(goes[side])(lambda side=side: tab_copy(side).wait_send())
        if wide:
            def sent(side=side):
                for c in range(CHUNKS):
                    to_relay(side, c).wait_send()
                direct(side, half).wait_send()

            when(goes[side], edge_out[side])(sent)
            when(goes[side], jnp.logical_not(edge_out[side]))(
                lambda side=side: direct(side, rows).wait_send()
            )

            def passed(side=side):
                for c in range(CHUNKS):
                    from_relay(side, c).wait_send()

            when(relays[side])(passed)
        else:
            when(goes[side])(lambda side=side: direct(side, rows).wait_send())


def fill_field(groups, plane, knots, base, local, basis, store):
    for group in range(groups):
        first = group * GROUP * (knots - 3) // plane
        value = spread(local, first) * basis[group * WINDOW]
        for i in range(1, WINDOW):
            value += spread(local, first + i) * basis[group * WINDOW + i]
        store(group, value + base)


def project_kernel(
    plane, knots, cap, table, rigid, local, basis, weight, pull, image_sum, slope_sum,
    grads, field, landed, moved,
):
    groups = plane // GROUP
    rows = plane // LANES
    sub, lane = grid_iota()
    field[0:FRONT, :] = jnp.zeros((FRONT, LANES), jnp.float32)
    field[FRONT + rows : FRONT + rows + BACK, :] = jnp.zeros((BACK, LANES), jnp.float32)
    clear(landed)
    clear(moved)
    base = shift_step * rigid[0].astype(jnp.float32)

    def store(group, value):
        field[FRONT + group * SUB : FRONT + (group + 1) * SUB, :] = value

    fill_field(groups, plane, knots, base, local, basis, store)

    for side in range(3):

        def body(pair, _):
            at_pair = side * cap + pair
            low, row_b, row_a, turn = pair_place(table, side, pair)
            keep = lane < LANES - turn
            slot = pair & 1
            for i in range(SPAN):
                at = pl.ds(pl.multiple_of(row_b + i * SUB, SUB), SUB)
                here = pl.ds(i * SUB, SUB)
                moved[slot, pl.ds(SUB + i * SUB, SUB), :] = (
                    image_sum[at_pair, here, :] + field[at, :] * slope_sum[at_pair, here, :]
                )
            for i in range(SPAN + 1):
                term = jnp.where(
                    keep,
                    moved[slot, pl.ds(SUB + i * SUB, SUB), :],
                    moved[slot, pl.ds(SUB + i * SUB - 1, SUB), :],
                )
                landed[side, pl.ds(row_a + i * SUB, SUB), :] += pltpu.roll(term, turn, 1)
            return 0

        lax.fori_loop(0, cap, body, 0)

    def own(group, _):
        at = pl.ds(pl.multiple_of(FRONT + group * SUB, SUB), SUB)
        here = pl.ds(pl.multiple_of(group * SUB, SUB), SUB)
        landed[1, at, :] = landed[1, at, :] - pull[here, :] - weight[here, :] * field[at, :]
        return 0

    lax.fori_loop(0, groups, own, 0, unroll=4)
    holders = [[] for _ in range(knots)]
    for group in range(groups):
        first = group * GROUP * (knots - 3) // plane
        for i in range(WINDOW):
            if first + i < knots:
                holders[first + i].append((group, group * WINDOW + i))
    for q, side in enumerate((1, 0, 2)):
        parts = []
        for j in range(knots):
            total = None
            for group, at in holders[j]:
                term = basis[at] * landed[side, FRONT + group * SUB : FRONT + (group + 1) * SUB, :]
                total = term if total is None else total + term
            parts.append(total)
        parts = [row_sums(parts[j : j + SUB]) for j in range(0, knots, SUB)]
        sums = jnp.concatenate(parts, axis=0)
        line = lanes_dot(jnp.ones((SUB, LANES), jnp.float32), sums)
        grads[q : q + 1, :] = -line[0:1, :]
    grads[3:SUB, :] = jnp.zeros((SUB - 3, LANES), jnp.float32)


def settle_kernel(
    tile_count, knot_count, block, blocks, mine, chosen, factors, coef, penalty,
    coef_out, local, own_out, work, *share_refs,
):
    greet(tile_count, knot_count)
    shared, finish = share(tile_count, knot_count, mine, share_refs)
    sums = shared[...]
    own, lower, upper = sums[:, 0, :], sums[:, 1, :], sums[:, 2, :]
    none = jnp.zeros((1, LANES), jnp.float32)
    grads = (
        own
        + jnp.concatenate([lower[1:, :], none], axis=0)
        + jnp.concatenate([none, upper[:-1, :]], axis=0)
    )
    grad_sum = cols_dot(halves(grads, block), chosen[...])
    bend = jnp.dot(
        penalty[...], coef[...], precision=HIGHEST, preferred_element_type=jnp.float32
    )
    work[...] = -(grad_sum + smooth_weight * bend)
    forward = []
    for k in range(block):
        value = spread(work, k)
        for back in (3, 2, 1):
            if k >= back:
                value = value - factors[back - 1, k] * forward[k - back]
        forward.append(value)
    steps = [None] * block
    for k in reversed(range(block)):
        value = forward[k] * factors[3, k]
        for ahead in (3, 2, 1):
            if k + ahead < block:
                value = value - factors[ahead - 1, k + ahead] * steps[k + ahead]
        steps[k] = value
        work[k : k + 1, :] = value[0:1, :]
    fresh = coef[...] + work[...]
    coef_out[...] = fresh
    spread_coef(blocks, fresh, local)
    lane = lax.broadcasted_iota(jnp.int32, (SUB, LANES), 1)
    me = lax.axis_index("tile") * knot_count + lax.axis_index("knot")
    own_out[...] = lanes_dot((lane == me).astype(jnp.float32), fresh)
    finish()


def warp_kernel(plane, knots, depth, rigid, local, basis, image, slope, out):
    step = pl.program_id(0)
    base = shift_step * rigid[0].astype(jnp.float32)
    count = basis.shape[0] // WINDOW

    def body(at, _):
        first = first_knot(step * count + at, plane, knots)
        value = jnp.zeros((SUB, LANES), jnp.float32)
        for i in range(WINDOW):
            value += jnp.broadcast_to(local[pl.ds(first + i, 1), :], (SUB, LANES)) * basis[
                at * WINDOW + i
            ]
        value += base
        for r in range(SUB):
            row = at * SUB + r
            out[row] = image[row] + slope[row] * value[r : r + 1, :]
        return 0

    lax.fori_loop(0, count, body, 0, unroll=2)


def per_device(images, gradient, shifts, tile_blocks, intersections, start_coefficients):
    depth, plane = images.shape[1:]
    block = start_coefficients.shape[1]
    knots = 2 * block
    groups = plane // GROUP
    rows = plane // LANES
    padded = FRONT + rows + BACK
    tile_count = lax.axis_size("tile")
    knot_count = lax.axis_size("knot")
    cap = intersections.shape[2]
    side = math.isqrt(tile_count // 2)
    wide = 2 * side if side > 1 and 2 * side * side == tile_count else 0

    def flat(volume):
        return volume.reshape(depth, rows, LANES).transpose(1, 0, 2)

    image, slope = flat(images[0]), flat(gradient[0])
    volume = pltpu.VMEM((padded, SUB, LANES), jnp.float32)
    pair_of = pltpu.SemaphoreType.DMA((2,))
    chunk_of = pltpu.SemaphoreType.DMA((CHUNKS,))

    basis, weight, pull, below, above, factors, chosen, coef, local = pl.pallas_call(
        functools.partial(
            begin_kernel, depth, plane, block, tile_count, knot_count, cap, wide
        ),
        out_shape=(
            f32(groups * WINDOW, SUB, LANES),
            f32(rows, LANES),
            f32(rows, LANES),
            f32(rows, SUB, LANES),
            f32(rows, SUB, LANES),
            f32(4, block, SUB, LANES),
            f32(2 * tile_count, LANES),
            f32(block, LANES),
            f32(knots + SUB, LANES),
        ),
        in_specs=[SMEM, SMEM, VMEM, ANY, ANY],
        out_specs=(VMEM,) * 3 + (ANY,) * 2 + (VMEM,) * 4,
        scratch_shapes=[
            pltpu.VMEM((rows, SUB, LANES), jnp.float32),
            pltpu.VMEM((rows, SUB, LANES), jnp.float32),
            pltpu.VMEM((rows // 2, SUB, LANES), jnp.float32),
            pltpu.VMEM((3, 2 * cap, LANES), jnp.float32),
            pltpu.VMEM((2, 2 * cap, LANES), jnp.float32),
            pltpu.VMEM((BAND, knots + SUB, SUB, LANES), jnp.float32),
            pltpu.VMEM((BAND, block, LANES), jnp.float32),
            pltpu.VMEM((2 * SUB, LANES), jnp.float32),
            pair_of, pair_of, pair_of, pair_of, pair_of,
            chunk_of, chunk_of, chunk_of, chunk_of,
            *share_scratch(tile_count, knot_count, 2 * SUB),
        ],
        compiler_params=pltpu.CompilerParams(
            collective_id=0, has_side_effects=True, vmem_limit_bytes=48 * 1024 * 1024
        ),
        name="begin",
    )(tile_blocks, intersections, start_coefficients, image, slope)
    image_sum, slope_sum = pl.pallas_call(
        functools.partial(pair_kernel, rows, cap),
        out_shape=(f32(3 * cap, SPAN * SUB, LANES),) * 2,
        in_specs=[SMEM] + [ANY] * 4,
        out_specs=(VMEM,) * 2,
        scratch_shapes=[volume] * 4 + [pltpu.SemaphoreType.DMA((4,))],
        compiler_params=pltpu.CompilerParams(vmem_limit_bytes=48 * 1024 * 1024),
        name="pairs",
    )(intersections, image, slope, below, above)
    penalty = jnp.asarray(smoothing(block))

    for step in range(ITERS):
        grads = pl.pallas_call(
            functools.partial(project_kernel, plane, knots, cap),
            out_shape=f32(SUB, LANES),
            in_specs=[SMEM] * 2 + [VMEM] * 6,
            out_specs=VMEM,
            scratch_shapes=[
                pltpu.VMEM((padded, LANES), jnp.float32),
                pltpu.VMEM((3, padded, LANES), jnp.float32),
                pltpu.VMEM((2, (SPAN + 3) * SUB, LANES), jnp.float32),
            ],
            compiler_params=PARAMS,
            name="project",
        )(intersections, shifts, local, basis, weight, pull, image_sum, slope_sum)
        coef, local, own = pl.pallas_call(
            functools.partial(settle_kernel, tile_count, knot_count, block),
            out_shape=(f32(block, LANES), f32(knots + SUB, LANES), f32(SUB, block)),
            in_specs=[SMEM] + [VMEM] * 5,
            out_specs=(VMEM,) * 3,
            scratch_shapes=[
                pltpu.VMEM((block, LANES), jnp.float32),
                *share_scratch(tile_count, knot_count, SUB),
            ],
            compiler_params=pltpu.CompilerParams(
                collective_id=1, has_side_effects=True, vmem_limit_bytes=16 * 1024 * 1024
            ),
            name="settle",
        )(tile_blocks, grads, chosen, factors, coef, penalty)

    cuts = 8
    part = pl.BlockSpec((rows // cuts, SUB, LANES), lambda i: (i, 0, 0))
    warped = pl.pallas_call(
        functools.partial(warp_kernel, plane, knots, depth),
        out_shape=f32(rows, depth, LANES),
        grid=(cuts,),
        in_specs=[
            SMEM,
            pl.BlockSpec((knots + SUB, LANES), lambda i: (0, 0)),
            pl.BlockSpec((groups * WINDOW // cuts, SUB, LANES), lambda i: (i, 0, 0)),
            part,
            part,
        ],
        out_specs=part,
        compiler_params=pltpu.CompilerParams(vmem_limit_bytes=56 * 1024 * 1024),
        name="warp",
    )(shifts, local, basis, image, slope)
    return own[0:1], warped.transpose(1, 0, 2).reshape(1, depth, plane)


def solution(mesh):
    placed = (
        P("tile", "knot", None),
        P("tile", "knot", None),
        P("tile"),
        P("tile", None),
        P("tile", None, None, None),
        P(("tile", "knot"), None),
    )
    return jax.shard_map(
        per_device,
        mesh=mesh,
        in_specs=placed,
        out_specs=(P(("tile", "knot"), None), P("tile", "knot", None)),
        check_vma=False,
    )
```

```python
import functools
import math

import jax
import jax.numpy as jnp
import numpy as np
from jax import lax
from jax.experimental import pallas as pl
from jax.experimental.pallas import tpu as pltpu
from jax.sharding import PartitionSpec as P

SLAB = 8192
ITERS = 2
LANES = 128
SUB = 8
GROUP = SUB * LANES
FRONT = 8
BACK = 16
WINDOW = 6
BAND = 4
CHUNKS = 4
CUTS = 8
SPAN = SLAB // GROUP + 1

shift_step = 0.05
smooth_weight = 20.0
ridge_weight = 1.0
HIGHEST = lax.Precision.HIGHEST
MESH = pl.DeviceIdType.MESH
VMEM = pl.BlockSpec(memory_space=pltpu.VMEM)
SMEM = pl.BlockSpec(memory_space=pltpu.SMEM)
ANY = pl.BlockSpec(memory_space=pl.ANY)
PARAMS = pltpu.CompilerParams(vmem_limit_bytes=16 * 1024 * 1024)


def f32(*shape):
    return jax.ShapeDtypeStruct(shape, jnp.float32)


def smoothing(block):
    second = np.zeros((block - 2, block), np.float32)
    for row in range(block - 2):
        second[row, row : row + 3] = (1.0, -2.0, 1.0)
    return second.T @ second


def cols_dot(left, right):
    return lax.dot_general(
        left, right, (((0,), (0,)), ((), ())), precision=HIGHEST,
        preferred_element_type=jnp.float32,
    )


def lanes_dot(left, right):
    return lax.dot_general(
        left, right, (((1,), (1,)), ((), ())), precision=HIGHEST,
        preferred_element_type=jnp.float32,
    )


def grid_iota():
    sub = lax.broadcasted_iota(jnp.int32, (SUB, LANES), 0)
    lane = lax.broadcasted_iota(jnp.int32, (SUB, LANES), 1)
    return sub, lane


def first_knot(group, plane, knots):
    return lax.div(group * (GROUP * (knots - 3)), plane)


def clear(ref):
    ref[...] = jnp.zeros(ref.shape, ref.dtype)


def lane_sums(partial):
    return lanes_dot(jnp.ones((SUB, LANES), jnp.float32), jnp.sum(partial, axis=1))[0:1, :]


def row_sums(values):
    sub = lax.broadcasted_iota(jnp.int32, (SUB, LANES), 0)
    for bit in (1, 2, 4):
        low = (sub & bit) == 0
        values = [
            jnp.where(low, a, b) + pltpu.roll(jnp.where(low, b, a), bit, 0)
            for a, b in zip(values[0::2], values[1::2])
        ]
    return values[0]


def spread(ref, row):
    return jnp.broadcast_to(ref[row : row + 1, :], (SUB, LANES))


def greet(tile_count, knot_count, between=None):
    tile, knot = lax.axis_index("tile"), lax.axis_index("knot")
    barrier = pltpu.get_barrier_semaphore()
    for step in range(1, knot_count):
        pl.semaphore_signal(
            barrier, inc=1, device_id=(tile, lax.rem(knot + step, knot_count)), device_id_type=MESH
        )

    def call(step, _):
        pl.semaphore_signal(
            barrier, inc=1, device_id=(lax.rem(tile + step, tile_count), knot), device_id_type=MESH
        )
        return 0

    lax.fori_loop(1, tile_count, call, 0)
    if between is not None:
        between()
    pl.semaphore_wait(barrier, tile_count + knot_count - 2)


def share_scratch(tile_count, knot_count, rows):
    return [
        pltpu.VMEM((rows, LANES), jnp.float32),
        pltpu.VMEM((knot_count, rows, LANES), jnp.float32),
        pltpu.VMEM((tile_count, rows, LANES), jnp.float32),
        pltpu.SemaphoreType.DMA((knot_count,)),
        pltpu.SemaphoreType.DMA((knot_count,)),
        pltpu.SemaphoreType.DMA((tile_count,)),
        pltpu.SemaphoreType.DMA((tile_count,)),
    ]


def share(tile_count, knot_count, mine, scratch, between=None):
    total, column, table, send_a, recv_a, send_b, recv_b = scratch
    tile, knot = lax.axis_index("tile"), lax.axis_index("knot")

    def over_knot(step, slot):
        return pltpu.make_async_remote_copy(
            src_ref=mine,
            dst_ref=column.at[slot],
            send_sem=send_a.at[step],
            recv_sem=recv_a.at[slot],
            device_id=(tile, lax.rem(knot + step, knot_count)),
            device_id_type=MESH,
        )

    def over_tile(step, slot):
        return pltpu.make_async_remote_copy(
            src_ref=total,
            dst_ref=table.at[slot],
            send_sem=send_b.at[step],
            recv_sem=recv_b.at[slot],
            device_id=(lax.rem(tile + step, tile_count), knot),
            device_id_type=MESH,
        )

    for step in range(1, knot_count):
        over_knot(step, knot).start()
    column[knot] = mine[...]
    if between is not None:
        between()
    for step in range(1, knot_count):
        over_knot(step, lax.rem(knot + step, knot_count)).wait_recv()
    total[...] = jnp.sum(column[...], axis=0)

    def send(step, _):
        over_tile(step, tile).start()
        return 0

    lax.fori_loop(1, tile_count, send, 0)
    table[tile] = total[...]

    def arrived():
        def arrive(step, _):
            over_tile(step, lax.rem(tile + step, tile_count)).wait_recv()
            return 0

        lax.fori_loop(1, tile_count, arrive, 0)
        return table

    def finish():
        for step in range(1, knot_count):
            over_knot(step, knot).wait_send()

        def sent(step, _):
            over_tile(step, tile).wait_send()
            return 0

        lax.fori_loop(1, tile_count, sent, 0)

    return arrived, finish


def halves(value, block):
    return jnp.concatenate([value[:, 0:block], value[:, block : 2 * block]], axis=0)


def spread_coef(blocks, coef, out):
    block = coef.shape[0]
    sub = lax.broadcasted_iota(jnp.int32, (LANES, LANES), 0)
    for n in range(2):
        hot = (sub == blocks[0, n]).astype(jnp.float32)
        out[n * block : (n + 1) * block, :] = jnp.dot(
            coef, hot, precision=HIGHEST, preferred_element_type=jnp.float32
        )
    out[2 * block : 2 * block + SUB, :] = jnp.zeros((SUB, LANES), jnp.float32)


def factor(block, penalty, system, factors):
    def entry(k, d):
        extra = smooth_weight * float(penalty[k - d, k]) + (ridge_weight if d == 0 else 0.0)
        return spread(system.at[d], k - d) + extra

    zero = jnp.zeros((SUB, LANES), jnp.float32)
    rows = []
    for k in range(block):
        p1, q1, r1, i1 = rows[k - 1] if k >= 1 else (zero,) * 4
        p2, q2, r2, i2 = rows[k - 2] if k >= 2 else (zero,) * 4
        p3, q3, r3, i3 = rows[k - 3] if k >= 3 else (zero,) * 4
        ur = entry(k, 3) if k >= 3 else zero
        uq = entry(k, 2) - ur * p2 if k >= 2 else zero
        up = entry(k, 1) - ur * q1 - uq * p1 if k >= 1 else zero
        r, q, p = ur * i3, uq * i2, up * i1
        inverse = 1.0 / (entry(k, 0) - ur * r - uq * q - up * p)
        rows.append((p, q, r, inverse))
        for which, value in enumerate((p, q, r, inverse)):
            factors[which, k] = value


def pair_place(table, side, pair):
    low = table[0, side, pair, 1] & (GROUP - 1)
    start = table[0, side, pair, 1] - low
    shift = table[0, side, pair, 3] - low
    row_b = pl.multiple_of(FRONT + lax.shift_right_logical(start, 7), SUB)
    row_a = FRONT + lax.shift_right_arithmetic(shift, 7)
    return low, row_b, row_a, shift & (LANES - 1)


def pair_sums(table, side, cap, far, image, slope, image_sum, slope_sum):
    sub, lane = grid_iota()
    place0 = sub * LANES + lane

    def body(at, _):
        pair = side * cap + at
        low, row_b, row_a, turn = pair_place(table, side, at)
        live = table[0, side, at, 4].astype(jnp.float32)
        back = (LANES - turn) & (LANES - 1)
        keep = lane >= turn
        for i in range(SPAN):
            c, d = [], []
            for r in range(SUB):
                row = i * SUB + r
                a = jnp.where(keep, far[row_a + row], far[row_a + (row + 1)])
                a = pltpu.roll(a, back, 1)
                c.append(a * image[row_b + row])
                d.append(a * slope[row_b + row])
            s = place0 + (i * GROUP - low)
            inside = (s >= 0) & (s < SLAB) & (live != 0.0)
            image_sum[pair, pl.ds(i * SUB, SUB), :] = jnp.where(inside, row_sums(c) * live, 0.0)
            slope_sum[pair, pl.ds(i * SUB, SUB), :] = jnp.where(inside, row_sums(d) * live, 0.0)
        return 0

    lax.fori_loop(0, cap, body, 0)


def pair_kernel(
    rows, cap, table, image, slope, below, above, image_sum, slope_sum,
    own_image, own_slope, own_below, own_above, sem,
):
    middle = pl.ds(FRONT, rows)
    loads = [
        pltpu.make_async_copy(src, dst.at[middle], sem.at[i])
        for i, (src, dst) in enumerate(
            ((image, own_image), (slope, own_slope), (below, own_below), (above, own_above))
        )
    ]
    for load in loads:
        load.start()
    loads[0].wait()
    loads[1].wait()
    pair_sums(table, 1, cap, own_slope, own_image, own_slope, image_sum, slope_sum)
    loads[2].wait()
    pair_sums(table, 0, cap, own_below, own_image, own_slope, image_sum, slope_sum)
    loads[3].wait()
    pair_sums(table, 2, cap, own_above, own_image, own_slope, image_sum, slope_sum)


def begin_kernel(
    depth, plane, block, tile_count, knot_count, cap, wide,
    blocks, table, first_coef, image, slope,
    basis, weight, pull, below, above, bands, chosen, coef, local,
    own_image, own_slope, passing, tabs, tabs_in, acc, mine, first, heads, columns,
    here_sem, tab_send, tab_recv, big_send, big_recv, chunk_send, chunk_recv, pass_send, pass_recv,
    head_send, head_recv, column_send, column_recv,
    *share_refs,
):
    knots = 2 * block
    rows = plane // LANES
    groups = plane // GROUP
    half, piece = rows // 2, rows // 2 // CHUNKS
    tile, knot = lax.axis_index("tile"), lax.axis_index("knot")
    pos = lax.rem(tile, wide) if wide else tile
    sub, lane = grid_iota()
    place0 = sub * LANES + lane
    land = (below, above)
    loads = [
        pltpu.make_async_copy(image, own_image, here_sem.at[0]),
        pltpu.make_async_copy(slope, own_slope, here_sem.at[1]),
    ]
    for load in loads:
        load.start()
    for d in range(3):
        for m in range(cap):
            for row, part in ((m, 3), (cap + m, 4)):
                value = table[0, d, m, part].astype(jnp.float32)
                tabs[d, row : row + 1, :] = jnp.full((1, LANES), value)
    lane_row = lax.broadcasted_iota(jnp.int32, (1, LANES), 1)
    clear(first)
    first[0:1, 0:block] = first_coef[...]
    first[1:2, :] = jnp.where(
        lane_row == 0,
        blocks[0, 0].astype(jnp.float32),
        jnp.where(lane_row == 1, blocks[0, 1].astype(jnp.float32), 0.0),
    )
    heads[tile] = first[...]
    greet(tile_count, knot_count)

    def head_copy(step, slot):
        return pltpu.make_async_remote_copy(
            src_ref=first, dst_ref=heads.at[slot],
            send_sem=head_send.at[step], recv_sem=head_recv.at[slot],
            device_id=(lax.rem(tile + step, tile_count), knot), device_id_type=MESH,
        )

    def column_copy(step, slot):
        return pltpu.make_async_remote_copy(
            src_ref=heads, dst_ref=columns.at[slot],
            send_sem=column_send.at[step], recv_sem=column_recv.at[slot],
            device_id=(tile, lax.rem(knot + step, knot_count)), device_id_type=MESH,
        )

    def each(count, act):
        def body(step, _):
            act(step)
            return 0

        lax.fori_loop(1, count, body, 0)

    def remote(src, dst, send_sem, recv_sem, to):
        return pltpu.make_async_remote_copy(
            src_ref=src, dst_ref=dst, send_sem=send_sem, recv_sem=recv_sem,
            device_id=(to, knot), device_id_type=MESH,
        )

    def tab_copy(side):
        return remote(
            tabs.at[2 - 2 * side], tabs_in.at[side], tab_send.at[side], tab_recv.at[side],
            tile + (1 - 2 * side),
        )

    def direct(side, count):
        return remote(
            slope.at[pl.ds(0, count)], land[side].at[pl.ds(0, count)],
            big_send.at[side], big_recv.at[side], tile + (1 - 2 * side),
        )

    def to_relay(side, c):
        return remote(
            slope.at[pl.ds(half + c * piece, piece)], passing.at[pl.ds(c * piece, piece)],
            chunk_send.at[c], chunk_recv.at[c], tile + (wide - 2 * wide * side),
        )

    def from_relay(side, c):
        return remote(
            passing.at[pl.ds(c * piece, piece)],
            land[side].at[pl.ds(half + c * piece, piece)],
            pass_send.at[c], pass_recv.at[c], tile + (1 - wide if side == 0 else wide - 1),
        )

    goes = (tile + 1 < tile_count, tile > 0)
    comes = (tile > 0, tile + 1 < tile_count)
    if wide:
        edge_out = (pos == wide - 1, pos == 0)
        edge_in = (pos == 0, pos == wide - 1)
        relays = ((pos == wide - 1) & (tile >= wide), (pos == 0) & (tile + wide < tile_count))

    def when(*terms):
        flag = terms[0]
        for term in terms[1:]:
            flag = flag & term
        return pl.when(flag)

    for side in range(2):
        when(goes[side])(lambda side=side: tab_copy(side).start())
    each(tile_count, lambda step: head_copy(step, tile).start())
    for side in range(2):
        if wide:
            def split(side=side):
                for c in range(CHUNKS):
                    to_relay(side, c).start()
                direct(side, half).start()

            when(goes[side], edge_out[side])(split)
            when(goes[side], jnp.logical_not(edge_out[side]))(
                lambda side=side: direct(side, rows).start()
            )
        else:
            when(goes[side])(lambda side=side: direct(side, rows).start())

    def forward(c):
        if wide:
            for side in range(2):
                def hand_on(side=side):
                    to_relay(side, c).wait_recv()
                    from_relay(side, c).start()

                when(relays[side])(hand_on)

    clear(acc)
    for load in loads:
        load.wait()

    def squares(group, _):
        gg, gi = [], []
        for r in range(SUB):
            row = group * SUB + r
            g = own_slope[row]
            gg.append(g * g)
            gi.append(g * own_image[row])
        here = pl.ds(pl.multiple_of(group * SUB, SUB), SUB)
        weight[here, :] = row_sums(gg)
        pull[here, :] = row_sums(gi)
        return 0

    lax.fori_loop(0, groups, squares, 0)
    forward(0)
    for side in range(2):
        when(comes[side])(lambda side=side: tab_copy(side).wait_recv())

        def absent(side=side):
            tabs_in[side] = jnp.zeros((2 * cap, LANES), jnp.float32)

        when(jnp.logical_not(comes[side]))(absent)

    def body(group, _):
        here = pl.ds(pl.multiple_of(group * SUB, SUB), SUB)
        at = (place0 + group * GROUP).astype(jnp.float32)
        count = jnp.zeros((SUB, LANES), jnp.float32)
        for source in (tabs_in.at[0], tabs.at[1], tabs_in.at[1]):
            for m in range(cap):
                s = at - spread(source, m)
                inside = (s >= 0.0) & (s < float(SLAB))
                count += jnp.where(inside, spread(source, cap + m), 0.0)
        w = weight[here, :] * count
        weight[here, :] = w
        pull[here, :] = pull[here, :] * count
        knot0 = first_knot(group, plane, knots)
        place = at * ((knots - 3) / plane) + 1.0
        parts = []
        for i in range(WINDOW):
            dist = jnp.abs(place - (knot0 + i).astype(jnp.float32))
            inner = 2.0 / 3.0 - dist * dist + 0.5 * dist * dist * dist
            outer = (2.0 - dist) * (2.0 - dist) * (2.0 - dist) * (1.0 / 6.0)
            value = jnp.where(dist < 1.0, inner, jnp.where(dist < 2.0, outer, 0.0))
            basis[group * WINDOW + i] = value
            parts.append(value)
        for i in range(WINDOW):
            scaled = parts[i] * w
            for d in range(min(BAND, WINDOW - i)):
                acc[d, knot0 + i] += scaled * parts[i + d]
        return 0

    lax.fori_loop(0, groups // 2, body, 0)
    forward(1)
    lax.fori_loop(groups // 2, groups, body, 0)
    forward(2)
    clear(mine)
    for d in range(BAND):
        mine[d : d + 1, :] = lane_sums(acc[d, 0:knots])
    each(tile_count, lambda step: head_copy(step, lax.rem(tile + step, tile_count)).wait_recv())
    each(knot_count, lambda step: column_copy(step, knot).start())
    columns[knot] = heads[...]
    forward(3)
    arrived, finish = share(tile_count, knot_count, mine, share_refs)
    each(
        knot_count,
        lambda step: column_copy(step, lax.rem(knot + step, knot_count)).wait_recv(),
    )
    labels = heads[:, 1, :]
    labels = jnp.concatenate([labels[:, 0:1], labels[:, 1:2]], axis=0)
    wide_lane = lax.broadcasted_iota(jnp.int32, (2 * tile_count, LANES), 1).astype(jnp.float32)
    chosen[...] = (wide_lane == labels).astype(jnp.float32)
    row = lax.broadcasted_iota(jnp.int32, (tile_count, LANES), 0) * knot_count
    col = lax.broadcasted_iota(jnp.int32, (tile_count, LANES), 1)
    start = jnp.zeros((block, LANES), jnp.float32)
    for k in range(knot_count):
        start += cols_dot(columns[k, :, 0, 0:block], (row + k == col).astype(jnp.float32))
    coef[...] = start
    spread_coef(blocks, start, local)

    for side in range(2):
        if wide:
            def pieces(side=side):
                direct(side, half).wait_recv()
                for c in range(CHUNKS):
                    from_relay(side, c).wait_recv()

            when(comes[side], edge_in[side])(pieces)
            when(comes[side], jnp.logical_not(edge_in[side]))(
                lambda side=side: direct(side, rows).wait_recv()
            )
        else:
            when(comes[side])(lambda side=side: direct(side, rows).wait_recv())
    bands[...] = arrived()[...]
    finish()
    each(tile_count, lambda step: head_copy(step, tile).wait_send())
    each(knot_count, lambda step: column_copy(step, knot).wait_send())
    for side in range(2):
        when(goes[side])(lambda side=side: tab_copy(side).wait_send())
        if wide:
            def sent(side=side):
                for c in range(CHUNKS):
                    to_relay(side, c).wait_send()
                direct(side, half).wait_send()

            when(goes[side], edge_out[side])(sent)
            when(goes[side], jnp.logical_not(edge_out[side]))(
                lambda side=side: direct(side, rows).wait_send()
            )

            def passed(side=side):
                for c in range(CHUNKS):
                    from_relay(side, c).wait_send()

            when(relays[side])(passed)
        else:
            when(goes[side])(lambda side=side: direct(side, rows).wait_send())


def fill_field(groups, plane, knots, base, local, basis, store):
    for group in range(groups):
        first = group * GROUP * (knots - 3) // plane
        value = spread(local, first) * basis[group * WINDOW]
        for i in range(1, WINDOW):
            value += spread(local, first + i) * basis[group * WINDOW + i]
        store(group, value + base)


def project_kernel(
    plane, knots, cap, table, rigid, local, basis, weight, pull, image_sum, slope_sum,
    landed, field, moved,
):
    groups = plane // GROUP
    rows = plane // LANES
    sub, lane = grid_iota()
    field[0:FRONT, :] = jnp.zeros((FRONT, LANES), jnp.float32)
    field[FRONT + rows : FRONT + rows + BACK, :] = jnp.zeros((BACK, LANES), jnp.float32)
    clear(landed)
    clear(moved)
    base = shift_step * rigid[0].astype(jnp.float32)

    def store(group, value):
        field[FRONT + group * SUB : FRONT + (group + 1) * SUB, :] = value

    fill_field(groups, plane, knots, base, local, basis, store)

    for side in range(3):

        def body(pair, _):
            at_pair = side * cap + pair
            low, row_b, row_a, turn = pair_place(table, side, pair)
            keep = lane < LANES - turn
            slot = pair & 1
            for i in range(SPAN):
                at = pl.ds(pl.multiple_of(row_b + i * SUB, SUB), SUB)
                here = pl.ds(i * SUB, SUB)
                moved[slot, pl.ds(SUB + i * SUB, SUB), :] = (
                    image_sum[at_pair, here, :] + field[at, :] * slope_sum[at_pair, here, :]
                )
            for i in range(SPAN + 1):
                term = jnp.where(
                    keep,
                    moved[slot, pl.ds(SUB + i * SUB, SUB), :],
                    moved[slot, pl.ds(SUB + i * SUB - 1, SUB), :],
                )
                landed[side, pl.ds(row_a + i * SUB, SUB), :] += pltpu.roll(term, turn, 1)
            return 0

        lax.fori_loop(0, cap, body, 0)

    def own(group, _):
        at = pl.ds(pl.multiple_of(FRONT + group * SUB, SUB), SUB)
        here = pl.ds(pl.multiple_of(group * SUB, SUB), SUB)
        landed[1, at, :] = landed[1, at, :] - pull[here, :] - weight[here, :] * field[at, :]
        return 0

    lax.fori_loop(0, groups, own, 0, unroll=4)


def project(groups, plane, knots, basis, landed, grads):
    holders = [[] for _ in range(knots)]
    for group in range(groups):
        first = group * GROUP * (knots - 3) // plane
        for i in range(WINDOW):
            if first + i < knots:
                holders[first + i].append((group, group * WINDOW + i))
    for q, side in enumerate((1, 0, 2)):
        parts = []
        for j in range(knots):
            total = None
            for group, at in holders[j]:
                term = basis[at] * landed[side, FRONT + group * SUB : FRONT + (group + 1) * SUB, :]
                total = term if total is None else total + term
            parts.append(total)
        parts = [row_sums(parts[j : j + SUB]) for j in range(0, knots, SUB)]
        sums = jnp.concatenate(parts, axis=0)
        line = lanes_dot(jnp.ones((SUB, LANES), jnp.float32), sums)
        grads[q : q + 1, :] = -line[0:1, :]
    grads[3:SUB, :] = jnp.zeros((SUB - 3, LANES), jnp.float32)


def settle_kernel(
    tile_count, knot_count, block, plane, opening, blocks, landed, basis, chosen, given, coef,
    penalty, coef_out, local, own_out, *refs,
):
    if opening:
        factors, work, mine, system, *share_refs = refs
    else:
        factors, (work, mine, *share_refs) = given, refs

    def gather():
        project(plane // GROUP, plane, 2 * block, basis, landed, mine)

    def prepare():
        if opening:
            select = chosen[...]
            bands = given[...]
            for d in range(BAND):
                system[d] = cols_dot(halves(bands[:, d, :], block), select)
            factor(block, smoothing(block), system, factors)

    greet(tile_count, knot_count, gather)
    arrived, finish = share(tile_count, knot_count, mine, share_refs, prepare)
    sums = arrived()[...]
    own, lower, upper = sums[:, 0, :], sums[:, 1, :], sums[:, 2, :]
    none = jnp.zeros((1, LANES), jnp.float32)
    grads = (
        own
        + jnp.concatenate([lower[1:, :], none], axis=0)
        + jnp.concatenate([none, upper[:-1, :]], axis=0)
    )
    grad_sum = cols_dot(halves(grads, block), chosen[...])
    bend = jnp.dot(
        penalty[...], coef[...], precision=HIGHEST, preferred_element_type=jnp.float32
    )
    work[...] = -(grad_sum + smooth_weight * bend)
    forward = []
    for k in range(block):
        value = spread(work, k)
        for back in (3, 2, 1):
            if k >= back:
                value = value - factors[back - 1, k] * forward[k - back]
        forward.append(value)
    steps = [None] * block
    for k in reversed(range(block)):
        value = forward[k] * factors[3, k]
        for ahead in (3, 2, 1):
            if k + ahead < block:
                value = value - factors[ahead - 1, k + ahead] * steps[k + ahead]
        steps[k] = value
        work[k : k + 1, :] = value[0:1, :]
    fresh = coef[...] + work[...]
    coef_out[...] = fresh
    spread_coef(blocks, fresh, local)
    lane = lax.broadcasted_iota(jnp.int32, (SUB, LANES), 1)
    me = lax.axis_index("tile") * knot_count + lax.axis_index("knot")
    own_out[...] = lanes_dot((lane == me).astype(jnp.float32), fresh)
    finish()


def warp_kernel(
    plane, knots, rigid, local, basis, image, slope, out, own_image, own_slope, field, load_sem, save_sem
):
    groups = plane // GROUP
    rows = plane // LANES
    part = rows // CUTS
    base = shift_step * rigid[0].astype(jnp.float32)

    def load(which, cut):
        src, dst = ((image, own_image), (slope, own_slope))[which]
        here = pl.ds(cut * part, part)
        return pltpu.make_async_copy(src.at[here], dst.at[here], load_sem.at[which, cut])

    def save(cut):
        here = pl.ds(cut * part, part)
        return pltpu.make_async_copy(own_image.at[here], out.at[here], save_sem.at[cut])

    for cut in range(CUTS):
        for which in range(2):
            load(which, cut).start()

    def store(group, value):
        field[group * SUB : (group + 1) * SUB, :] = value

    fill_field(groups, plane, knots, base, local, basis, store)
    for cut in range(CUTS):
        for which in range(2):
            load(which, cut).wait()

        def body(group, _):
            for r in range(SUB):
                row = group * SUB + r
                shift = jnp.broadcast_to(field[pl.ds(row, 1), :], (SUB, LANES))
                own_image[row] = own_image[row] + own_slope[row] * shift
            return 0

        lax.fori_loop(cut * (groups // CUTS), (cut + 1) * (groups // CUTS), body, 0, unroll=2)
        save(cut).start()
    for cut in range(CUTS):
        save(cut).wait()


def per_device(images, gradient, shifts, tile_blocks, intersections, start_coefficients):
    depth, plane = images.shape[1:]
    block = start_coefficients.shape[1]
    knots = 2 * block
    groups = plane // GROUP
    rows = plane // LANES
    padded = FRONT + rows + BACK
    tile_count = lax.axis_size("tile")
    knot_count = lax.axis_size("knot")
    cap = intersections.shape[2]
    side = math.isqrt(tile_count // 2)
    wide = 2 * side if side > 1 and 2 * side * side == tile_count else 0

    def flat(volume):
        return volume.reshape(depth, rows, LANES).transpose(1, 0, 2)

    image, slope = flat(images[0]), flat(gradient[0])
    volume = pltpu.VMEM((padded, SUB, LANES), jnp.float32)
    pair_of = pltpu.SemaphoreType.DMA((2,))
    chunk_of = pltpu.SemaphoreType.DMA((CHUNKS,))

    basis, weight, pull, below, above, bands, chosen, coef, local = pl.pallas_call(
        functools.partial(
            begin_kernel, depth, plane, block, tile_count, knot_count, cap, wide
        ),
        out_shape=(
            f32(groups * WINDOW, SUB, LANES),
            f32(rows, LANES),
            f32(rows, LANES),
            f32(rows, SUB, LANES),
            f32(rows, SUB, LANES),
            f32(tile_count, SUB, LANES),
            f32(2 * tile_count, LANES),
            f32(block, LANES),
            f32(knots + SUB, LANES),
        ),
        in_specs=[SMEM, SMEM, VMEM, ANY, ANY],
        out_specs=(VMEM,) * 3 + (ANY,) * 2 + (VMEM,) * 4,
        scratch_shapes=[
            pltpu.VMEM((rows, SUB, LANES), jnp.float32),
            pltpu.VMEM((rows, SUB, LANES), jnp.float32),
            pltpu.VMEM((rows // 2, SUB, LANES), jnp.float32),
            pltpu.VMEM((3, 2 * cap, LANES), jnp.float32),
            pltpu.VMEM((2, 2 * cap, LANES), jnp.float32),
            pltpu.VMEM((BAND, knots + SUB, SUB, LANES), jnp.float32),
            pltpu.VMEM((SUB, LANES), jnp.float32),
            pltpu.VMEM((SUB, LANES), jnp.float32),
            pltpu.VMEM((tile_count, SUB, LANES), jnp.float32),
            pltpu.VMEM((knot_count, tile_count, SUB, LANES), jnp.float32),
            pair_of, pair_of, pair_of, pair_of, pair_of,
            chunk_of, chunk_of, chunk_of, chunk_of,
            pltpu.SemaphoreType.DMA((tile_count,)),
            pltpu.SemaphoreType.DMA((tile_count,)),
            pltpu.SemaphoreType.DMA((knot_count,)),
            pltpu.SemaphoreType.DMA((knot_count,)),
            *share_scratch(tile_count, knot_count, SUB),
        ],
        compiler_params=pltpu.CompilerParams(
            collective_id=0, has_side_effects=True, vmem_limit_bytes=48 * 1024 * 1024
        ),
        name="begin",
    )(tile_blocks, intersections, start_coefficients, image, slope)
    image_sum, slope_sum = pl.pallas_call(
        functools.partial(pair_kernel, rows, cap),
        out_shape=(f32(3 * cap, SPAN * SUB, LANES),) * 2,
        in_specs=[SMEM] + [ANY] * 4,
        out_specs=(VMEM,) * 2,
        scratch_shapes=[volume] * 4 + [pltpu.SemaphoreType.DMA((4,))],
        compiler_params=pltpu.CompilerParams(vmem_limit_bytes=16 * 1024 * 1024),
        name="pairs",
    )(intersections, image, slope, below, above)
    penalty = jnp.asarray(smoothing(block))

    factors = bands
    for step in range(ITERS):
        opening = step == 0
        landed = pl.pallas_call(
            functools.partial(project_kernel, plane, knots, cap),
            out_shape=f32(3, padded, LANES),
            in_specs=[SMEM] * 2 + [VMEM] * 6,
            out_specs=VMEM,
            scratch_shapes=[
                pltpu.VMEM((padded, LANES), jnp.float32),
                pltpu.VMEM((2, (SPAN + 3) * SUB, LANES), jnp.float32),
            ],
            compiler_params=PARAMS,
            name="project",
        )(intersections, shifts, local, basis, weight, pull, image_sum, slope_sum)
        outs = (f32(block, LANES), f32(knots + SUB, LANES), f32(SUB, block))
        if opening:
            outs += (f32(4, block, SUB, LANES),)
        coef, local, own, *made = pl.pallas_call(
            functools.partial(settle_kernel, tile_count, knot_count, block, plane, opening),
            out_shape=outs,
            in_specs=[SMEM] + [VMEM] * 6,
            out_specs=(VMEM,) * len(outs),
            scratch_shapes=[
                pltpu.VMEM((block, LANES), jnp.float32),
                pltpu.VMEM((SUB, LANES), jnp.float32),
                *([pltpu.VMEM((BAND, block, LANES), jnp.float32)] if opening else []),
                *share_scratch(tile_count, knot_count, SUB),
            ],
            compiler_params=pltpu.CompilerParams(
                collective_id=1 if opening else 2,
                has_side_effects=True,
                vmem_limit_bytes=16 * 1024 * 1024,
            ),
            name="settle_first" if opening else "settle",
        )(tile_blocks, landed, basis, chosen, factors, coef, penalty)
        if opening:
            factors = made[0]

    whole = pltpu.VMEM((rows, SUB, LANES), jnp.float32)
    warped = pl.pallas_call(
        functools.partial(warp_kernel, plane, knots),
        out_shape=f32(rows, depth, LANES),
        in_specs=[SMEM, VMEM, VMEM, ANY, ANY],
        out_specs=ANY,
        scratch_shapes=[
            whole,
            whole,
            pltpu.VMEM((rows, LANES), jnp.float32),
            pltpu.SemaphoreType.DMA((2, CUTS)),
            pltpu.SemaphoreType.DMA((CUTS,)),
        ],
        compiler_params=PARAMS,
        name="warp",
    )(shifts, local, basis, image, slope)
    return own[0:1], warped.transpose(1, 0, 2).reshape(1, depth, plane)


def solution(mesh):
    placed = (
        P("tile", "knot", None),
        P("tile", "knot", None),
        P("tile"),
        P("tile", None),
        P("tile", None, None, None),
        P(("tile", "knot"), None),
    )
    return jax.shard_map(
        per_device,
        mesh=mesh,
        in_specs=placed,
        out_specs=(P(("tile", "knot"), None), P("tile", "knot", None)),
        check_vma=False,
    )
```

```python
import functools
import math

import jax
import jax.numpy as jnp
import numpy as np
from jax import lax
from jax.experimental import pallas as pl
from jax.experimental.pallas import tpu as pltpu
from jax.sharding import PartitionSpec as P

SLAB = 8192
ITERS = 2
LANES = 128
SUB = 8
GROUP = SUB * LANES
FRONT = 8
BACK = 16
WINDOW = 6
BAND = 4
CHUNKS = 4
REACH = WINDOW + 1
SPOTS = 24
CUTS = 8
SPAN = SLAB // GROUP + 1

shift_step = 0.05
smooth_weight = 20.0
ridge_weight = 1.0
HIGHEST = lax.Precision.HIGHEST
MESH = pl.DeviceIdType.MESH
VMEM = pl.BlockSpec(memory_space=pltpu.VMEM)
SMEM = pl.BlockSpec(memory_space=pltpu.SMEM)
ANY = pl.BlockSpec(memory_space=pl.ANY)
PARAMS = pltpu.CompilerParams(vmem_limit_bytes=16 * 1024 * 1024)


def f32(*shape):
    return jax.ShapeDtypeStruct(shape, jnp.float32)


def smoothing(block):
    second = np.zeros((block - 2, block), np.float32)
    for row in range(block - 2):
        second[row, row : row + 3] = (1.0, -2.0, 1.0)
    return second.T @ second


def cols_dot(left, right):
    return lax.dot_general(
        left, right, (((0,), (0,)), ((), ())), precision=HIGHEST,
        preferred_element_type=jnp.float32,
    )


def lanes_dot(left, right):
    return lax.dot_general(
        left, right, (((1,), (1,)), ((), ())), precision=HIGHEST,
        preferred_element_type=jnp.float32,
    )


def spline(offset):
    dist = jnp.abs(offset)
    inner = 2.0 / 3.0 - dist * dist + 0.5 * dist * dist * dist
    outer = (2.0 - dist) * (2.0 - dist) * (2.0 - dist) * (1.0 / 6.0)
    return jnp.where(dist < 1.0, inner, jnp.where(dist < 2.0, outer, 0.0))


def grid_iota():
    sub = lax.broadcasted_iota(jnp.int32, (SUB, LANES), 0)
    lane = lax.broadcasted_iota(jnp.int32, (SUB, LANES), 1)
    return sub, lane


def first_knot(group, plane, knots):
    return lax.div(group * (GROUP * (knots - 3)), plane)


def clear(ref):
    ref[...] = jnp.zeros(ref.shape, ref.dtype)


def lane_sums(partial):
    return lanes_dot(jnp.ones((SUB, LANES), jnp.float32), jnp.sum(partial, axis=1))[0:1, :]


def row_sums(values):
    sub = lax.broadcasted_iota(jnp.int32, (SUB, LANES), 0)
    for bit in (1, 2, 4):
        low = (sub & bit) == 0
        values = [
            jnp.where(low, a, b) + pltpu.roll(jnp.where(low, b, a), bit, 0)
            for a, b in zip(values[0::2], values[1::2])
        ]
    return values[0]


def spread(ref, row):
    return jnp.broadcast_to(ref[row : row + 1, :], (SUB, LANES))


def greet(tile_count, knot_count, between=None):
    tile, knot = lax.axis_index("tile"), lax.axis_index("knot")
    barrier = pltpu.get_barrier_semaphore()
    for step in range(1, knot_count):
        pl.semaphore_signal(
            barrier, inc=1, device_id=(tile, lax.rem(knot + step, knot_count)), device_id_type=MESH
        )

    def call(step, _):
        pl.semaphore_signal(
            barrier, inc=1, device_id=(lax.rem(tile + step, tile_count), knot), device_id_type=MESH
        )
        return 0

    lax.fori_loop(1, tile_count, call, 0)
    if between is not None:
        between()
    pl.semaphore_wait(barrier, tile_count + knot_count - 2)


def share_scratch(tile_count, knot_count, rows):
    return [
        pltpu.VMEM((rows, LANES), jnp.float32),
        pltpu.VMEM((knot_count, rows, LANES), jnp.float32),
        pltpu.VMEM((tile_count, rows, LANES), jnp.float32),
        pltpu.SemaphoreType.DMA((knot_count,)),
        pltpu.SemaphoreType.DMA((knot_count,)),
        pltpu.SemaphoreType.DMA((tile_count,)),
        pltpu.SemaphoreType.DMA((tile_count,)),
    ]


def share(tile_count, knot_count, mine, scratch):
    total, column, table, send_a, recv_a, send_b, recv_b = scratch
    tile, knot = lax.axis_index("tile"), lax.axis_index("knot")

    def over_knot(step, slot):
        return pltpu.make_async_remote_copy(
            src_ref=mine,
            dst_ref=column.at[slot],
            send_sem=send_a.at[step],
            recv_sem=recv_a.at[slot],
            device_id=(tile, lax.rem(knot + step, knot_count)),
            device_id_type=MESH,
        )

    def over_tile(step, slot):
        return pltpu.make_async_remote_copy(
            src_ref=total,
            dst_ref=table.at[slot],
            send_sem=send_b.at[step],
            recv_sem=recv_b.at[slot],
            device_id=(lax.rem(tile + step, tile_count), knot),
            device_id_type=MESH,
        )

    def each(count, act):
        def body(step, _):
            act(step)
            return 0

        lax.fori_loop(1, count, body, 0)

    def open_knot():
        each(knot_count, lambda step: over_knot(step, knot).start())
        column[knot] = mine[...]

    def open_tile():
        each(knot_count, lambda step: over_knot(step, lax.rem(knot + step, knot_count)).wait_recv())
        total[...] = jnp.sum(column[...], axis=0)
        each(tile_count, lambda step: over_tile(step, tile).start())
        table[tile] = total[...]

    def arrived():
        each(tile_count, lambda step: over_tile(step, lax.rem(tile + step, tile_count)).wait_recv())
        return table[...]

    def finish():
        each(knot_count, lambda step: over_knot(step, knot).wait_send())
        each(tile_count, lambda step: over_tile(step, tile).wait_send())

    return open_knot, open_tile, arrived, finish


def halves(value, block):
    return jnp.concatenate([value[:, 0:block], value[:, block : 2 * block]], axis=0)


def spread_coef(blocks, coef, out):
    block = coef.shape[0]
    sub = lax.broadcasted_iota(jnp.int32, (LANES, LANES), 0)
    for n in range(2):
        hot = (sub == blocks[0, n]).astype(jnp.float32)
        out[n * block : (n + 1) * block, :] = jnp.dot(
            coef, hot, precision=HIGHEST, preferred_element_type=jnp.float32
        )
    out[2 * block : 2 * block + SUB, :] = jnp.zeros((SUB, LANES), jnp.float32)


def factor(block, penalty, system, factors):
    def entry(k, d):
        extra = smooth_weight * float(penalty[k - d, k]) + (ridge_weight if d == 0 else 0.0)
        return spread(system.at[d], k - d) + extra

    zero = jnp.zeros((SUB, LANES), jnp.float32)
    rows = []
    for k in range(block):
        p1, q1, r1, i1 = rows[k - 1] if k >= 1 else (zero,) * 4
        p2, q2, r2, i2 = rows[k - 2] if k >= 2 else (zero,) * 4
        p3, q3, r3, i3 = rows[k - 3] if k >= 3 else (zero,) * 4
        ur = entry(k, 3) if k >= 3 else zero
        uq = entry(k, 2) - ur * p2 if k >= 2 else zero
        up = entry(k, 1) - ur * q1 - uq * p1 if k >= 1 else zero
        r, q, p = ur * i3, uq * i2, up * i1
        inverse = 1.0 / (entry(k, 0) - ur * r - uq * q - up * p)
        rows.append((p, q, r, inverse))
        for which, value in enumerate((p, q, r, inverse)):
            factors[which, k] = value


def pair_place(table, side, pair):
    low = table[0, side, pair, 1] & (GROUP - 1)
    start = table[0, side, pair, 1] - low
    shift = table[0, side, pair, 3] - low
    row_b = pl.multiple_of(FRONT + lax.shift_right_logical(start, 7), SUB)
    row_a = FRONT + lax.shift_right_arithmetic(shift, 7)
    return low, row_b, row_a, shift & (LANES - 1)


def pair_sums(table, side, cap, far, image, slope, image_sum, slope_sum):
    sub, lane = grid_iota()
    place0 = sub * LANES + lane

    def body(at, _):
        pair = side * cap + at
        low, row_b, row_a, turn = pair_place(table, side, at)
        live = table[0, side, at, 4].astype(jnp.float32)
        back = (LANES - turn) & (LANES - 1)
        keep = lane >= turn
        for i in range(SPAN):
            c, d = [], []
            for r in range(SUB):
                row = i * SUB + r
                a = jnp.where(keep, far[row_a + row], far[row_a + (row + 1)])
                a = pltpu.roll(a, back, 1)
                c.append(a * image[row_b + row])
                d.append(a * slope[row_b + row])
            s = place0 + (i * GROUP - low)
            inside = (s >= 0) & (s < SLAB) & (live != 0.0)
            image_sum[pair, pl.ds(i * SUB, SUB), :] = jnp.where(inside, row_sums(c) * live, 0.0)
            slope_sum[pair, pl.ds(i * SUB, SUB), :] = jnp.where(inside, row_sums(d) * live, 0.0)
        return 0

    lax.fori_loop(0, cap, body, 0)


def pair_kernel(
    rows, cap, table, image, slope, below, above, image_sum, slope_sum,
    own_image, own_slope, own_below, own_above, sem,
):
    middle = pl.ds(FRONT, rows)
    loads = [
        pltpu.make_async_copy(src, dst.at[middle], sem.at[i])
        for i, (src, dst) in enumerate(
            ((image, own_image), (slope, own_slope), (below, own_below), (above, own_above))
        )
    ]
    for load in loads:
        load.start()
    loads[0].wait()
    loads[1].wait()
    pair_sums(table, 1, cap, own_slope, own_image, own_slope, image_sum, slope_sum)
    loads[2].wait()
    pair_sums(table, 0, cap, own_below, own_image, own_slope, image_sum, slope_sum)
    loads[3].wait()
    pair_sums(table, 2, cap, own_above, own_image, own_slope, image_sum, slope_sum)


def begin_kernel(
    depth, plane, block, tile_count, knot_count, cap, wide,
    blocks, table, first_coef, image, slope,
    basis, weight, pull, below, above, bands, chosen, coef, local, shapes, spots,
    own_image, own_slope, passing, tabs, tabs_in, acc, first, heads, columns,
    here_sem, tab_send, tab_recv, big_send, big_recv, chunk_send, chunk_recv, pass_send, pass_recv,
    head_send, head_recv, column_send, column_recv,
):
    knots = 2 * block
    rows = plane // LANES
    groups = plane // GROUP
    half, piece = rows // 2, rows // 2 // CHUNKS
    tile, knot = lax.axis_index("tile"), lax.axis_index("knot")
    pos = lax.rem(tile, wide) if wide else tile
    sub, lane = grid_iota()
    place0 = sub * LANES + lane
    land = (below, above)
    loads = [
        pltpu.make_async_copy(image, own_image, here_sem.at[0]),
        pltpu.make_async_copy(slope, own_slope, here_sem.at[1]),
    ]
    for load in loads:
        load.start()
    for d in range(3):
        for m in range(cap):
            for row, part in ((m, 3), (cap + m, 4)):
                value = table[0, d, m, part].astype(jnp.float32)
                tabs[d, row : row + 1, :] = jnp.full((1, LANES), value)
    lane_row = lax.broadcasted_iota(jnp.int32, (1, LANES), 1)
    clear(first)
    first[0:1, 0:block] = first_coef[...]
    first[1:2, :] = jnp.where(
        lane_row == 0,
        blocks[0, 0].astype(jnp.float32),
        jnp.where(lane_row == 1, blocks[0, 1].astype(jnp.float32), 0.0),
    )
    heads[tile] = first[...]
    greet(tile_count, knot_count)

    def head_copy(step, slot):
        return pltpu.make_async_remote_copy(
            src_ref=first, dst_ref=heads.at[slot],
            send_sem=head_send.at[step], recv_sem=head_recv.at[slot],
            device_id=(lax.rem(tile + step, tile_count), knot), device_id_type=MESH,
        )

    def column_copy(step, slot):
        return pltpu.make_async_remote_copy(
            src_ref=heads, dst_ref=columns.at[slot],
            send_sem=column_send.at[step], recv_sem=column_recv.at[slot],
            device_id=(tile, lax.rem(knot + step, knot_count)), device_id_type=MESH,
        )

    def each(count, act):
        def body(step, _):
            act(step)
            return 0

        lax.fori_loop(1, count, body, 0)

    def remote(src, dst, send_sem, recv_sem, to):
        return pltpu.make_async_remote_copy(
            src_ref=src, dst_ref=dst, send_sem=send_sem, recv_sem=recv_sem,
            device_id=(to, knot), device_id_type=MESH,
        )

    def tab_copy(side):
        return remote(
            tabs.at[2 - 2 * side], tabs_in.at[side], tab_send.at[side], tab_recv.at[side],
            tile + (1 - 2 * side),
        )

    def direct(side, c):
        return remote(
            slope.at[pl.ds(c * piece, piece)], land[side].at[pl.ds(c * piece, piece)],
            big_send.at[side, c], big_recv.at[side, c], tile + (1 - 2 * side),
        )

    def to_relay(side, c):
        return remote(
            slope.at[pl.ds(half + c * piece, piece)], passing.at[pl.ds(c * piece, piece)],
            chunk_send.at[c], chunk_recv.at[c], tile + (wide - 2 * wide * side),
        )

    def from_relay(side, c):
        return remote(
            passing.at[pl.ds(c * piece, piece)],
            land[side].at[pl.ds(half + c * piece, piece)],
            pass_send.at[c], pass_recv.at[c], tile + (1 - wide if side == 0 else wide - 1),
        )

    goes = (tile + 1 < tile_count, tile > 0)
    comes = (tile > 0, tile + 1 < tile_count)
    if wide:
        edge_out = (pos == wide - 1, pos == 0)
        edge_in = (pos == 0, pos == wide - 1)
        relays = ((pos == wide - 1) & (tile >= wide), (pos == 0) & (tile + wide < tile_count))

    def when(*terms):
        flag = terms[0]
        for term in terms[1:]:
            flag = flag & term
        return pl.when(flag)

    for side in range(2):
        when(goes[side])(lambda side=side: tab_copy(side).start())
    each(tile_count, lambda step: head_copy(step, tile).start())
    def for_pieces(order, flags, edges, plain, relayed):
        for c in order:
            for side in range(2):
                if wide and c >= CHUNKS:
                    when(flags[side], edges[side])(
                        lambda side=side, c=c: relayed(side, c - CHUNKS)
                    )
                    when(flags[side], jnp.logical_not(edges[side]))(
                        lambda side=side, c=c: plain(side, c)
                    )
                else:
                    when(flags[side])(lambda side=side, c=c: plain(side, c))

    order = [c for pair in zip(range(CHUNKS, 2 * CHUNKS), range(CHUNKS)) for c in pair]
    edges = edge_out if wide else None

    def launch(part):
        for_pieces(
            part, goes, edges,
            lambda side, c: direct(side, c).start(),
            lambda side, c: to_relay(side, c).start(),
        )

    launch(order[:2])
    each(tile_count, lambda step: head_copy(step, lax.rem(tile + step, tile_count)).wait_recv())
    each(knot_count, lambda step: column_copy(step, knot).start())
    launch(order[2:])
    columns[knot] = heads[...]

    def forward(c):
        if wide:
            for side in range(2):
                def hand_on(side=side):
                    to_relay(side, c).wait_recv()
                    from_relay(side, c).start()

                when(relays[side])(hand_on)

    clear(acc)
    for load in loads:
        load.wait()

    def squares(group, _):
        gg, gi = [], []
        for r in range(SUB):
            row = group * SUB + r
            g = own_slope[row]
            gg.append(g * g)
            gi.append(g * own_image[row])
        here = pl.ds(pl.multiple_of(group * SUB, SUB), SUB)
        weight[here, :] = row_sums(gg)
        pull[here, :] = row_sums(gi)
        return 0

    lax.fori_loop(0, groups, squares, 0)
    forward(0)
    for side in range(2):
        when(comes[side])(lambda side=side: tab_copy(side).wait_recv())

        def absent(side=side):
            tabs_in[side] = jnp.zeros((2 * cap, LANES), jnp.float32)

        when(jnp.logical_not(comes[side]))(absent)

    def body(group, _):
        here = pl.ds(pl.multiple_of(group * SUB, SUB), SUB)
        at = (place0 + group * GROUP).astype(jnp.float32)
        count = jnp.zeros((SUB, LANES), jnp.float32)
        for source in (tabs_in.at[0], tabs.at[1], tabs_in.at[1]):
            for m in range(cap):
                s = at - spread(source, m)
                inside = (s >= 0.0) & (s < float(SLAB))
                count += jnp.where(inside, spread(source, cap + m), 0.0)
        w = weight[here, :] * count
        weight[here, :] = w
        pull[here, :] = pull[here, :] * count
        knot0 = first_knot(group, plane, knots)
        place = at * ((knots - 3) / plane) + 1.0
        parts = []
        for i in range(WINDOW):
            value = spline(place - (knot0 + i).astype(jnp.float32))
            basis[group * WINDOW + i] = value
            parts.append(value)
        for i in range(WINDOW):
            scaled = parts[i] * w
            for d in range(min(BAND, WINDOW - i)):
                acc[d, knot0 + i] += scaled * parts[i + d]
        return 0

    lax.fori_loop(0, groups // 2, body, 0)
    forward(1)
    lax.fori_loop(groups // 2, groups, body, 0)
    forward(2)
    for d in range(BAND):
        bands[d : d + 1, :] = lane_sums(acc[d, 0:knots])
    bands[BAND:SUB, :] = jnp.zeros((SUB - BAND, LANES), jnp.float32)
    forward(3)
    each(
        knot_count,
        lambda step: column_copy(step, lax.rem(knot + step, knot_count)).wait_recv(),
    )
    labels = heads[:, 1, :]
    labels = jnp.concatenate([labels[:, 0:1], labels[:, 1:2]], axis=0)
    wide_lane = lax.broadcasted_iota(jnp.int32, (2 * tile_count, LANES), 1).astype(jnp.float32)
    chosen[...] = (wide_lane == labels).astype(jnp.float32)
    row = lax.broadcasted_iota(jnp.int32, (tile_count, LANES), 0) * knot_count
    col = lax.broadcasted_iota(jnp.int32, (tile_count, LANES), 1)
    start = jnp.zeros((block, LANES), jnp.float32)
    for k in range(knot_count):
        start += cols_dot(columns[k, :, 0, 0:block], (row + k == col).astype(jnp.float32))
    coef[...] = start
    spread_coef(blocks, start, local)

    for d in range(3):

        def shape(m, _):
            at_pair = d * cap + m
            low = table[0, d, m, 1] & (GROUP - 1)
            origin = table[0, d, m, 3] - low
            knot0 = (origin * (knots - 3)) >> (plane.bit_length() - 1)
            place = (place0 + origin).astype(jnp.float32)
            for i in range(SPAN):
                here = (place + float(i * GROUP)) * ((knots - 3) / plane) + 1.0
                for r in range(REACH):
                    j = knot0 + (i * GROUP * (knots - 3) // plane + r)
                    shapes[at_pair, i * REACH + r] = spline(here - j.astype(jnp.float32))
            row = lax.broadcasted_iota(jnp.int32, (SPOTS, LANES), 0)
            col = lax.broadcasted_iota(jnp.int32, (SPOTS, LANES), 1)
            spots[pl.ds(pl.multiple_of(at_pair * SPOTS, SUB), SPOTS), :] = (
                row + knot0 == col
            ).astype(jnp.float32)
            return 0

        lax.fori_loop(0, cap, shape, 0)

    for_pieces(
        order, comes, edge_in if wide else None,
        lambda side, c: direct(side, c).wait_recv(),
        lambda side, c: from_relay(side, c).wait_recv(),
    )
    each(tile_count, lambda step: head_copy(step, tile).wait_send())
    each(knot_count, lambda step: column_copy(step, knot).wait_send())
    for side in range(2):
        when(goes[side])(lambda side=side: tab_copy(side).wait_send())
    for_pieces(
        order, goes, edges,
        lambda side, c: direct(side, c).wait_send(),
        lambda side, c: to_relay(side, c).wait_send(),
    )
    if wide:
        for side in range(2):
            def passed(side=side):
                for c in range(CHUNKS):
                    from_relay(side, c).wait_send()

            when(relays[side])(passed)


def fill_field(groups, plane, knots, base, local, basis, store):
    for group in range(groups):
        first = group * GROUP * (knots - 3) // plane
        value = spread(local, first) * basis[group * WINDOW]
        for i in range(1, WINDOW):
            value += spread(local, first + i) * basis[group * WINDOW + i]
        store(group, value + base)


def refine_kernel(
    plane, tile_count, knot_count, block, cap,
    blocks, table, rigid, basis, weight, pull, image_sum, slope_sum, shapes, spots, bands, chosen,
    coef_in, local_in, penalty, local, own_out,
    field, coef, factors, system, work, marks, mine_first, mine_second, *share_refs,
):
    knots = 2 * block
    groups = plane // GROUP
    each = len(share_refs) // 3
    sets = [share_refs[n * each : (n + 1) * each] for n in range(3)]
    field[groups] = jnp.zeros((SUB, LANES), jnp.float32)
    base = shift_step * rigid[0].astype(jnp.float32)
    ones = jnp.ones((SUB, LANES), jnp.float32)
    local[...] = local_in[...]
    coef[...] = coef_in[...]
    holders = [[] for _ in range(knots)]
    for group in range(groups):
        first = group * GROUP * (knots - 3) // plane
        for i in range(WINDOW):
            if first + i < knots:
                holders[first + i].append((group, group * WINDOW + i))

    def store(group, value):
        field[group] = value

    def slabs():
        fill_field(groups, plane, knots, base, local, basis, store)
        for side in range(3):

            def body(m, _):
                pair = side * cap + m
                group = lax.shift_right_logical(table[0, side, m, 1], GROUP.bit_length() - 1)
                parts = [None] * SPOTS
                for i in range(SPAN):
                    here = pl.ds(i * SUB, SUB)
                    term = image_sum[pair, here, :] + slope_sum[pair, here, :] * field[group + i]
                    for r in range(REACH):
                        j = i * GROUP * (knots - 3) // plane + r
                        value = term * shapes[pair, i * REACH + r]
                        parts[j] = value if parts[j] is None else parts[j] + value
                zero = jnp.zeros((SUB, LANES), jnp.float32)
                parts = [zero if part is None else part for part in parts]
                for j in range(0, SPOTS, SUB):
                    marks[pl.ds(pl.multiple_of(pair * SPOTS + j, SUB), SUB), :] = row_sums(
                        parts[j : j + SUB]
                    )
                return 0

            lax.fori_loop(0, cap, body, 0)

    def gather(mine):
        for group in range(groups):
            here = slice(group * SUB, (group + 1) * SUB)
            field[group] = pull[here, :] + weight[here, :] * field[group]
        parts = []
        for j in range(knots):
            total = None
            for group, at in holders[j]:
                term = basis[at] * field[group]
                total = term if total is None else total + term
            parts.append(total)
        sums = jnp.concatenate(
            [row_sums(parts[j : j + SUB]) for j in range(0, knots, SUB)], axis=0
        )
        count = cap * SPOTS
        lines = []
        for side in range(3):
            at = slice(side * count, (side + 1) * count)
            values = lanes_dot(ones, marks[at, :])
            lines.append(
                -jnp.dot(
                    values, spots[at, :], precision=HIGHEST, preferred_element_type=jnp.float32
                )[0:1, :]
            )
        mine[0:1, :] = lanes_dot(ones, sums)[0:1, :] + lines[1]
        mine[1:2, :] = lines[0]
        mine[2:3, :] = lines[2]
        mine[3:SUB, :] = jnp.zeros((SUB - 3, LANES), jnp.float32)

    def solve(sums):
        own, lower, upper = sums[:, 0, :], sums[:, 1, :], sums[:, 2, :]
        none = jnp.zeros((1, LANES), jnp.float32)
        grads = (
            own
            + jnp.concatenate([lower[1:, :], none], axis=0)
            + jnp.concatenate([none, upper[:-1, :]], axis=0)
        )
        grad_sum = cols_dot(halves(grads, block), chosen[...])
        bend = jnp.dot(
            penalty[...], coef[...], precision=HIGHEST, preferred_element_type=jnp.float32
        )
        work[...] = -(grad_sum + smooth_weight * bend)
        forward = []
        for k in range(block):
            value = spread(work, k)
            for back in (3, 2, 1):
                if k >= back:
                    value = value - factors[back - 1, k] * forward[k - back]
            forward.append(value)
        steps = [None] * block
        for k in reversed(range(block)):
            value = forward[k] * factors[3, k]
            for ahead in (3, 2, 1):
                if k + ahead < block:
                    value = value - factors[ahead - 1, k + ahead] * steps[k + ahead]
            steps[k] = value
            work[k : k + 1, :] = value[0:1, :]
        coef[...] = coef[...] + work[...]
        spread_coef(blocks, coef[...], local)

    greet(tile_count, knot_count, slabs)
    band_knot, band_tile, band_table, band_finish = share(tile_count, knot_count, bands, sets[0])
    band_knot()
    open_knot, open_tile, arrived, finish_first = share(
        tile_count, knot_count, mine_first, sets[1]
    )
    gather(mine_first)
    open_knot()
    band_tile()
    open_tile()
    table_of = band_table()
    select = chosen[...]
    for d in range(BAND):
        system[d] = cols_dot(halves(table_of[:, d, :], block), select)
    factor(block, smoothing(block), system, factors)
    solve(arrived())
    slabs()
    gather(mine_second)
    open_knot, open_tile, arrived, finish_second = share(
        tile_count, knot_count, mine_second, sets[2]
    )
    open_knot()
    open_tile()
    solve(arrived())
    lane = lax.broadcasted_iota(jnp.int32, (SUB, LANES), 1)
    me = lax.axis_index("tile") * knot_count + lax.axis_index("knot")
    own_out[...] = lanes_dot((lane == me).astype(jnp.float32), coef[...])
    band_finish()
    finish_first()
    finish_second()


def warp_kernel(
    plane, knots, rigid, local, basis, image, slope, out, own_image, own_slope, field, load_sem, save_sem
):
    groups = plane // GROUP
    rows = plane // LANES
    part = rows // CUTS
    base = shift_step * rigid[0].astype(jnp.float32)

    def load(which, cut):
        src, dst = ((image, own_image), (slope, own_slope))[which]
        here = pl.ds(cut * part, part)
        return pltpu.make_async_copy(src.at[here], dst.at[here], load_sem.at[which, cut])

    def save(cut):
        here = pl.ds(cut * part, part)
        return pltpu.make_async_copy(own_image.at[here], out.at[here], save_sem.at[cut])

    for cut in range(CUTS):
        for which in range(2):
            load(which, cut).start()

    def store(group, value):
        field[group * SUB : (group + 1) * SUB, :] = value

    fill_field(groups, plane, knots, base, local, basis, store)
    for cut in range(CUTS):
        for which in range(2):
            load(which, cut).wait()

        def body(group, _):
            for r in range(SUB):
                row = group * SUB + r
                shift = jnp.broadcast_to(field[pl.ds(row, 1), :], (SUB, LANES))
                own_image[row] = own_image[row] + own_slope[row] * shift
            return 0

        lax.fori_loop(cut * (groups // CUTS), (cut + 1) * (groups // CUTS), body, 0, unroll=2)
        save(cut).start()
    for cut in range(CUTS):
        save(cut).wait()


def per_device(images, gradient, shifts, tile_blocks, intersections, start_coefficients):
    depth, plane = images.shape[1:]
    block = start_coefficients.shape[1]
    knots = 2 * block
    groups = plane // GROUP
    rows = plane // LANES
    padded = FRONT + rows + BACK
    tile_count = lax.axis_size("tile")
    knot_count = lax.axis_size("knot")
    cap = intersections.shape[2]
    side = math.isqrt(tile_count // 2)
    wide = 2 * side if side > 1 and 2 * side * side == tile_count else 0

    def flat(volume):
        return volume.reshape(depth, rows, LANES).transpose(1, 0, 2)

    image, slope = flat(images[0]), flat(gradient[0])
    volume = pltpu.VMEM((padded, SUB, LANES), jnp.float32)
    pair_of = pltpu.SemaphoreType.DMA((2,))
    piece_of = pltpu.SemaphoreType.DMA((2, 2 * CHUNKS))
    chunk_of = pltpu.SemaphoreType.DMA((CHUNKS,))

    basis, weight, pull, below, above, bands, chosen, coef, local, shapes, spots = pl.pallas_call(
        functools.partial(
            begin_kernel, depth, plane, block, tile_count, knot_count, cap, wide
        ),
        out_shape=(
            f32(groups * WINDOW, SUB, LANES),
            f32(rows, LANES),
            f32(rows, LANES),
            f32(rows, SUB, LANES),
            f32(rows, SUB, LANES),
            f32(SUB, LANES),
            f32(2 * tile_count, LANES),
            f32(block, LANES),
            f32(knots + SUB, LANES),
            f32(3 * cap, SPAN * REACH, SUB, LANES),
            f32(3 * cap * SPOTS, LANES),
        ),
        in_specs=[SMEM, SMEM, VMEM, ANY, ANY],
        out_specs=(VMEM,) * 3 + (ANY,) * 2 + (VMEM,) * 6,
        scratch_shapes=[
            pltpu.VMEM((rows, SUB, LANES), jnp.float32),
            pltpu.VMEM((rows, SUB, LANES), jnp.float32),
            pltpu.VMEM((rows // 2, SUB, LANES), jnp.float32),
            pltpu.VMEM((3, 2 * cap, LANES), jnp.float32),
            pltpu.VMEM((2, 2 * cap, LANES), jnp.float32),
            pltpu.VMEM((BAND, knots + SUB, SUB, LANES), jnp.float32),
            pltpu.VMEM((SUB, LANES), jnp.float32),
            pltpu.VMEM((tile_count, SUB, LANES), jnp.float32),
            pltpu.VMEM((knot_count, tile_count, SUB, LANES), jnp.float32),
            pair_of, pair_of, pair_of, piece_of, piece_of,
            chunk_of, chunk_of, chunk_of, chunk_of,
            pltpu.SemaphoreType.DMA((tile_count,)),
            pltpu.SemaphoreType.DMA((tile_count,)),
            pltpu.SemaphoreType.DMA((knot_count,)),
            pltpu.SemaphoreType.DMA((knot_count,)),
        ],
        compiler_params=pltpu.CompilerParams(
            collective_id=0, has_side_effects=True, vmem_limit_bytes=48 * 1024 * 1024
        ),
        name="begin",
    )(tile_blocks, intersections, start_coefficients, image, slope)
    image_sum, slope_sum = pl.pallas_call(
        functools.partial(pair_kernel, rows, cap),
        out_shape=(f32(3 * cap, SPAN * SUB, LANES),) * 2,
        in_specs=[SMEM] + [ANY] * 4,
        out_specs=(VMEM,) * 2,
        scratch_shapes=[volume] * 4 + [pltpu.SemaphoreType.DMA((4,))],
        compiler_params=pltpu.CompilerParams(vmem_limit_bytes=16 * 1024 * 1024),
        name="pairs",
    )(intersections, image, slope, below, above)
    penalty = jnp.asarray(smoothing(block))

    local, own = pl.pallas_call(
        functools.partial(refine_kernel, plane, tile_count, knot_count, block, cap),
        out_shape=(f32(knots + SUB, LANES), f32(SUB, block)),
        in_specs=[SMEM] * 3 + [VMEM] * 12,
        out_specs=(VMEM,) * 2,
        scratch_shapes=[
            pltpu.VMEM((groups + 1, SUB, LANES), jnp.float32),
            pltpu.VMEM((block, LANES), jnp.float32),
            pltpu.VMEM((4, block, SUB, LANES), jnp.float32),
            pltpu.VMEM((BAND, block, LANES), jnp.float32),
            pltpu.VMEM((block, LANES), jnp.float32),
            pltpu.VMEM((3 * cap * SPOTS, LANES), jnp.float32),
            pltpu.VMEM((SUB, LANES), jnp.float32),
            pltpu.VMEM((SUB, LANES), jnp.float32),
            *(share_scratch(tile_count, knot_count, SUB) * ITERS),
            *share_scratch(tile_count, knot_count, SUB),
        ],
        compiler_params=pltpu.CompilerParams(
            collective_id=1, has_side_effects=True, vmem_limit_bytes=24 * 1024 * 1024
        ),
        name="refine",
    )(
        tile_blocks, intersections, shifts, basis, weight, pull, image_sum, slope_sum, shapes,
        spots, bands, chosen, coef, local, penalty,
    )

    whole = pltpu.VMEM((rows, SUB, LANES), jnp.float32)
    warped = pl.pallas_call(
        functools.partial(warp_kernel, plane, knots),
        out_shape=f32(rows, depth, LANES),
        in_specs=[SMEM, VMEM, VMEM, ANY, ANY],
        out_specs=ANY,
        scratch_shapes=[
            whole,
            whole,
            pltpu.VMEM((rows, LANES), jnp.float32),
            pltpu.SemaphoreType.DMA((2, CUTS)),
            pltpu.SemaphoreType.DMA((CUTS,)),
        ],
        compiler_params=PARAMS,
        name="warp",
    )(shifts, local, basis, image, slope)
    return own[0:1], warped.transpose(1, 0, 2).reshape(1, depth, plane)


def solution(mesh):
    placed = (
        P("tile", "knot", None),
        P("tile", "knot", None),
        P("tile"),
        P("tile", None),
        P("tile", None, None, None),
        P(("tile", "knot"), None),
    )
    return jax.shard_map(
        per_device,
        mesh=mesh,
        in_specs=placed,
        out_specs=(P(("tile", "knot"), None), P("tile", "knot", None)),
        check_vma=False,
    )
```

```python
import functools
import math

import jax
import jax.numpy as jnp
import numpy as np
from jax import lax
from jax.experimental import pallas as pl
from jax.experimental.pallas import tpu as pltpu
from jax.sharding import PartitionSpec as P

SLAB = 8192
ITERS = 2
LANES = 128
SUB = 8
GROUP = SUB * LANES
FRONT = 8
BACK = 16
WINDOW = 6
BAND = 4
CHUNKS = 4
REACH = WINDOW + 1
SPOTS = 24
CUTS = 8
SPAN = SLAB // GROUP + 1

shift_step = 0.05
smooth_weight = 20.0
ridge_weight = 1.0
HIGHEST = lax.Precision.HIGHEST
MESH = pl.DeviceIdType.MESH
VMEM = pl.BlockSpec(memory_space=pltpu.VMEM)
SMEM = pl.BlockSpec(memory_space=pltpu.SMEM)
ANY = pl.BlockSpec(memory_space=pl.ANY)
PARAMS = pltpu.CompilerParams(vmem_limit_bytes=16 * 1024 * 1024)


def f32(*shape):
    return jax.ShapeDtypeStruct(shape, jnp.float32)


def smoothing(block):
    second = np.zeros((block - 2, block), np.float32)
    for row in range(block - 2):
        second[row, row : row + 3] = (1.0, -2.0, 1.0)
    return second.T @ second


def cols_dot(left, right):
    return lax.dot_general(
        left, right, (((0,), (0,)), ((), ())), precision=HIGHEST,
        preferred_element_type=jnp.float32,
    )


def lanes_dot(left, right):
    return lax.dot_general(
        left, right, (((1,), (1,)), ((), ())), precision=HIGHEST,
        preferred_element_type=jnp.float32,
    )


def spline(offset):
    dist = jnp.abs(offset)
    inner = 2.0 / 3.0 - dist * dist + 0.5 * dist * dist * dist
    outer = (2.0 - dist) * (2.0 - dist) * (2.0 - dist) * (1.0 / 6.0)
    return jnp.where(dist < 1.0, inner, jnp.where(dist < 2.0, outer, 0.0))


def grid_iota():
    sub = lax.broadcasted_iota(jnp.int32, (SUB, LANES), 0)
    lane = lax.broadcasted_iota(jnp.int32, (SUB, LANES), 1)
    return sub, lane


def first_knot(group, plane, knots):
    return lax.div(group * (GROUP * (knots - 3)), plane)


def clear(ref):
    ref[...] = jnp.zeros(ref.shape, ref.dtype)


def lane_sums(partial):
    return lanes_dot(jnp.ones((SUB, LANES), jnp.float32), jnp.sum(partial, axis=1))[0:1, :]


def row_sums(values):
    sub = lax.broadcasted_iota(jnp.int32, (SUB, LANES), 0)
    for bit in (1, 2, 4):
        low = (sub & bit) == 0
        values = [
            jnp.where(low, a, b) + pltpu.roll(jnp.where(low, b, a), bit, 0)
            for a, b in zip(values[0::2], values[1::2])
        ]
    return values[0]


def spread(ref, row):
    return jnp.broadcast_to(ref[row : row + 1, :], (SUB, LANES))


def greet(tile_count, knot_count, between=None):
    tile, knot = lax.axis_index("tile"), lax.axis_index("knot")
    barrier = pltpu.get_barrier_semaphore()
    for step in range(1, knot_count):
        pl.semaphore_signal(
            barrier, inc=1, device_id=(tile, lax.rem(knot + step, knot_count)), device_id_type=MESH
        )

    def call(step, _):
        pl.semaphore_signal(
            barrier, inc=1, device_id=(lax.rem(tile + step, tile_count), knot), device_id_type=MESH
        )
        return 0

    lax.fori_loop(1, tile_count, call, 0)
    if between is not None:
        between()
    pl.semaphore_wait(barrier, tile_count + knot_count - 2)


def share_scratch(tile_count, knot_count, rows):
    return [
        pltpu.VMEM((rows, LANES), jnp.float32),
        pltpu.VMEM((knot_count, rows, LANES), jnp.float32),
        pltpu.VMEM((tile_count, rows, LANES), jnp.float32),
        pltpu.SemaphoreType.DMA((knot_count,)),
        pltpu.SemaphoreType.DMA((knot_count,)),
        pltpu.SemaphoreType.DMA((tile_count,)),
        pltpu.SemaphoreType.DMA((tile_count,)),
    ]


def share(tile_count, knot_count, mine, scratch):
    total, column, table, send_a, recv_a, send_b, recv_b = scratch
    tile, knot = lax.axis_index("tile"), lax.axis_index("knot")

    def over_knot(step, slot):
        return pltpu.make_async_remote_copy(
            src_ref=mine,
            dst_ref=column.at[slot],
            send_sem=send_a.at[step],
            recv_sem=recv_a.at[slot],
            device_id=(tile, lax.rem(knot + step, knot_count)),
            device_id_type=MESH,
        )

    def over_tile(step, slot):
        return pltpu.make_async_remote_copy(
            src_ref=total,
            dst_ref=table.at[slot],
            send_sem=send_b.at[step],
            recv_sem=recv_b.at[slot],
            device_id=(lax.rem(tile + step, tile_count), knot),
            device_id_type=MESH,
        )

    def each(count, act):
        def body(step, _):
            act(step)
            return 0

        lax.fori_loop(1, count, body, 0)

    def open_knot():
        each(knot_count, lambda step: over_knot(step, knot).start())
        column[knot] = mine[...]

    def open_tile():
        each(knot_count, lambda step: over_knot(step, lax.rem(knot + step, knot_count)).wait_recv())
        total[...] = jnp.sum(column[...], axis=0)
        each(tile_count, lambda step: over_tile(step, tile).start())
        table[tile] = total[...]

    def arrived():
        each(tile_count, lambda step: over_tile(step, lax.rem(tile + step, tile_count)).wait_recv())
        return table[...]

    def finish():
        each(knot_count, lambda step: over_knot(step, knot).wait_send())
        each(tile_count, lambda step: over_tile(step, tile).wait_send())

    return open_knot, open_tile, arrived, finish


def halves(value, block):
    return jnp.concatenate([value[:, 0:block], value[:, block : 2 * block]], axis=0)


def spread_coef(blocks, coef, out):
    block = coef.shape[0]
    sub = lax.broadcasted_iota(jnp.int32, (LANES, LANES), 0)
    for n in range(2):
        hot = (sub == blocks[0, n]).astype(jnp.float32)
        out[n * block : (n + 1) * block, :] = jnp.dot(
            coef, hot, precision=HIGHEST, preferred_element_type=jnp.float32
        )
    out[2 * block : 2 * block + SUB, :] = jnp.zeros((SUB, LANES), jnp.float32)


def factor(block, penalty, system, factors):
    def entry(k, d):
        extra = smooth_weight * float(penalty[k - d, k]) + (ridge_weight if d == 0 else 0.0)
        return spread(system.at[d], k - d) + extra

    zero = jnp.zeros((SUB, LANES), jnp.float32)
    rows = []
    for k in range(block):
        p1, q1, r1, i1 = rows[k - 1] if k >= 1 else (zero,) * 4
        p2, q2, r2, i2 = rows[k - 2] if k >= 2 else (zero,) * 4
        p3, q3, r3, i3 = rows[k - 3] if k >= 3 else (zero,) * 4
        ur = entry(k, 3) if k >= 3 else zero
        uq = entry(k, 2) - ur * p2 if k >= 2 else zero
        up = entry(k, 1) - ur * q1 - uq * p1 if k >= 1 else zero
        r, q, p = ur * i3, uq * i2, up * i1
        inverse = 1.0 / (entry(k, 0) - ur * r - uq * q - up * p)
        rows.append((p, q, r, inverse))
        for which, value in enumerate((p, q, r, inverse)):
            factors[which, k] = value


def pair_place(table, side, pair):
    low = table[0, side, pair, 1] & (GROUP - 1)
    start = table[0, side, pair, 1] - low
    shift = table[0, side, pair, 3] - low
    row_b = pl.multiple_of(FRONT + lax.shift_right_logical(start, 7), SUB)
    row_a = FRONT + lax.shift_right_arithmetic(shift, 7)
    return low, row_b, row_a, shift & (LANES - 1)


def pair_sums(table, side, cap, far, image, slope, image_sum, slope_sum):
    sub, lane = grid_iota()
    place0 = sub * LANES + lane

    def body(at, _):
        pair = side * cap + at
        low, row_b, row_a, turn = pair_place(table, side, at)
        live = table[0, side, at, 4].astype(jnp.float32)
        back = (LANES - turn) & (LANES - 1)
        keep = lane >= turn
        for i in range(SPAN):
            c, d = [], []
            for r in range(SUB):
                row = i * SUB + r
                a = jnp.where(keep, far[row_a + row], far[row_a + (row + 1)])
                a = pltpu.roll(a, back, 1)
                c.append(a * image[row_b + row])
                d.append(a * slope[row_b + row])
            s = place0 + (i * GROUP - low)
            inside = (s >= 0) & (s < SLAB) & (live != 0.0)
            image_sum[pair, pl.ds(i * SUB, SUB), :] = jnp.where(inside, row_sums(c) * live, 0.0)
            slope_sum[pair, pl.ds(i * SUB, SUB), :] = jnp.where(inside, row_sums(d) * live, 0.0)
        return 0

    lax.fori_loop(0, cap, body, 0)


def pair_kernel(
    rows, cap, table, image, slope, below, above, image_sum, slope_sum,
    own_image, own_slope, own_below, own_above, sem,
):
    middle = pl.ds(FRONT, rows)
    loads = [
        pltpu.make_async_copy(src, dst.at[middle], sem.at[i])
        for i, (src, dst) in enumerate(
            ((image, own_image), (slope, own_slope), (below, own_below), (above, own_above))
        )
    ]
    for load in loads:
        load.start()
    loads[0].wait()
    loads[1].wait()
    pair_sums(table, 1, cap, own_slope, own_image, own_slope, image_sum, slope_sum)
    loads[2].wait()
    pair_sums(table, 0, cap, own_below, own_image, own_slope, image_sum, slope_sum)
    loads[3].wait()
    pair_sums(table, 2, cap, own_above, own_image, own_slope, image_sum, slope_sum)


def begin_kernel(
    depth, plane, block, tile_count, knot_count, cap, wide,
    blocks, table, first_coef, image, slope,
    basis, weight, pull, below, above, bands, chosen, coef, local, shapes, spots,
    own_image, own_slope, passing, tabs, tabs_in, acc, first, heads, columns,
    here_sem, tab_send, tab_recv, big_send, big_recv, chunk_send, chunk_recv, pass_send, pass_recv,
    head_send, head_recv, column_send, column_recv,
):
    knots = 2 * block
    rows = plane // LANES
    groups = plane // GROUP
    half, piece = rows // 2, rows // 2 // CHUNKS
    tile, knot = lax.axis_index("tile"), lax.axis_index("knot")
    pos = lax.rem(tile, wide) if wide else tile
    sub, lane = grid_iota()
    place0 = sub * LANES + lane
    land = (below, above)
    loads = [
        pltpu.make_async_copy(image, own_image, here_sem.at[0]),
        pltpu.make_async_copy(slope, own_slope, here_sem.at[1]),
    ]
    for load in loads:
        load.start()
    for d in range(3):
        for m in range(cap):
            for row, part in ((m, 3), (cap + m, 4)):
                value = table[0, d, m, part].astype(jnp.float32)
                tabs[d, row : row + 1, :] = jnp.full((1, LANES), value)
    lane_row = lax.broadcasted_iota(jnp.int32, (1, LANES), 1)
    clear(first)
    first[0:1, 0:block] = first_coef[...]
    first[1:2, :] = jnp.where(
        lane_row == 0,
        blocks[0, 0].astype(jnp.float32),
        jnp.where(lane_row == 1, blocks[0, 1].astype(jnp.float32), 0.0),
    )
    heads[tile] = first[...]
    greet(tile_count, knot_count)

    def head_copy(step, slot):
        return pltpu.make_async_remote_copy(
            src_ref=first, dst_ref=heads.at[slot],
            send_sem=head_send.at[step], recv_sem=head_recv.at[slot],
            device_id=(lax.rem(tile + step, tile_count), knot), device_id_type=MESH,
        )

    def column_copy(step, slot):
        return pltpu.make_async_remote_copy(
            src_ref=heads, dst_ref=columns.at[slot],
            send_sem=column_send.at[step], recv_sem=column_recv.at[slot],
            device_id=(tile, lax.rem(knot + step, knot_count)), device_id_type=MESH,
        )

    def each(count, act):
        def body(step, _):
            act(step)
            return 0

        lax.fori_loop(1, count, body, 0)

    def remote(src, dst, send_sem, recv_sem, to):
        return pltpu.make_async_remote_copy(
            src_ref=src, dst_ref=dst, send_sem=send_sem, recv_sem=recv_sem,
            device_id=(to, knot), device_id_type=MESH,
        )

    def tab_copy(side):
        return remote(
            tabs.at[2 - 2 * side], tabs_in.at[side], tab_send.at[side], tab_recv.at[side],
            tile + (1 - 2 * side),
        )

    def direct(side, c):
        return remote(
            slope.at[pl.ds(c * piece, piece)], land[side].at[pl.ds(c * piece, piece)],
            big_send.at[side, c], big_recv.at[side, c], tile + (1 - 2 * side),
        )

    def to_relay(side, c):
        return remote(
            slope.at[pl.ds(half + c * piece, piece)], passing.at[pl.ds(c * piece, piece)],
            chunk_send.at[c], chunk_recv.at[c], tile + (wide - 2 * wide * side),
        )

    def from_relay(side, c):
        return remote(
            passing.at[pl.ds(c * piece, piece)],
            land[side].at[pl.ds(half + c * piece, piece)],
            pass_send.at[c], pass_recv.at[c], tile + (1 - wide if side == 0 else wide - 1),
        )

    goes = (tile + 1 < tile_count, tile > 0)
    comes = (tile > 0, tile + 1 < tile_count)
    if wide:
        edge_out = (pos == wide - 1, pos == 0)
        edge_in = (pos == 0, pos == wide - 1)
        relays = ((pos == wide - 1) & (tile >= wide), (pos == 0) & (tile + wide < tile_count))

    def when(*terms):
        flag = terms[0]
        for term in terms[1:]:
            flag = flag & term
        return pl.when(flag)

    for side in range(2):
        when(goes[side])(lambda side=side: tab_copy(side).start())
    each(tile_count, lambda step: head_copy(step, tile).start())
    def for_pieces(order, flags, edges, plain, relayed):
        for c in order:
            for side in range(2):
                if wide and c >= CHUNKS:
                    when(flags[side], edges[side])(
                        lambda side=side, c=c: relayed(side, c - CHUNKS)
                    )
                    when(flags[side], jnp.logical_not(edges[side]))(
                        lambda side=side, c=c: plain(side, c)
                    )
                else:
                    when(flags[side])(lambda side=side, c=c: plain(side, c))

    order = [c for pair in zip(range(CHUNKS, 2 * CHUNKS), range(CHUNKS)) for c in pair]
    edges = edge_out if wide else None

    def launch(part):
        for_pieces(
            part, goes, edges,
            lambda side, c: direct(side, c).start(),
            lambda side, c: to_relay(side, c).start(),
        )

    launch(order[:2])
    each(tile_count, lambda step: head_copy(step, lax.rem(tile + step, tile_count)).wait_recv())
    each(knot_count, lambda step: column_copy(step, knot).start())
    launch(order[2:])
    columns[knot] = heads[...]

    def forward(c):
        if wide:
            for side in range(2):
                def hand_on(side=side):
                    to_relay(side, c).wait_recv()
                    from_relay(side, c).start()

                when(relays[side])(hand_on)

    clear(acc)
    for load in loads:
        load.wait()

    def squares(group, _):
        gg, gi = [], []
        for r in range(SUB):
            row = group * SUB + r
            g = own_slope[row]
            gg.append(g * g)
            gi.append(g * own_image[row])
        here = pl.ds(pl.multiple_of(group * SUB, SUB), SUB)
        weight[here, :] = row_sums(gg)
        pull[here, :] = row_sums(gi)
        return 0

    lax.fori_loop(0, groups, squares, 0)
    forward(0)
    for side in range(2):
        when(comes[side])(lambda side=side: tab_copy(side).wait_recv())

        def absent(side=side):
            tabs_in[side] = jnp.zeros((2 * cap, LANES), jnp.float32)

        when(jnp.logical_not(comes[side]))(absent)

    def body(group, _):
        here = pl.ds(pl.multiple_of(group * SUB, SUB), SUB)
        at = (place0 + group * GROUP).astype(jnp.float32)
        count = jnp.zeros((SUB, LANES), jnp.float32)
        for source in (tabs_in.at[0], tabs.at[1], tabs_in.at[1]):
            for m in range(cap):
                s = at - spread(source, m)
                inside = (s >= 0.0) & (s < float(SLAB))
                count += jnp.where(inside, spread(source, cap + m), 0.0)
        w = weight[here, :] * count
        weight[here, :] = w
        pull[here, :] = pull[here, :] * count
        knot0 = first_knot(group, plane, knots)
        place = at * ((knots - 3) / plane) + 1.0
        parts = []
        for i in range(WINDOW):
            value = spline(place - (knot0 + i).astype(jnp.float32))
            basis[group * WINDOW + i] = value
            parts.append(value)
        for i in range(WINDOW):
            scaled = parts[i] * w
            for d in range(min(BAND, WINDOW - i)):
                acc[d, knot0 + i] += scaled * parts[i + d]
        return 0

    lax.fori_loop(0, groups // 2, body, 0)
    forward(1)
    lax.fori_loop(groups // 2, groups, body, 0)
    forward(2)
    for d in range(BAND):
        bands[d : d + 1, :] = lane_sums(acc[d, 0:knots])
    bands[BAND:SUB, :] = jnp.zeros((SUB - BAND, LANES), jnp.float32)
    forward(3)
    each(
        knot_count,
        lambda step: column_copy(step, lax.rem(knot + step, knot_count)).wait_recv(),
    )
    labels = heads[:, 1, :]
    labels = jnp.concatenate([labels[:, 0:1], labels[:, 1:2]], axis=0)
    wide_lane = lax.broadcasted_iota(jnp.int32, (2 * tile_count, LANES), 1).astype(jnp.float32)
    chosen[...] = (wide_lane == labels).astype(jnp.float32)
    row = lax.broadcasted_iota(jnp.int32, (tile_count, LANES), 0) * knot_count
    col = lax.broadcasted_iota(jnp.int32, (tile_count, LANES), 1)
    start = jnp.zeros((block, LANES), jnp.float32)
    for k in range(knot_count):
        start += cols_dot(columns[k, :, 0, 0:block], (row + k == col).astype(jnp.float32))
    coef[...] = start
    spread_coef(blocks, start, local)

    for d in range(3):

        def shape(m, _):
            at_pair = d * cap + m
            low = table[0, d, m, 1] & (GROUP - 1)
            origin = table[0, d, m, 3] - low
            knot0 = (origin * (knots - 3)) >> (plane.bit_length() - 1)
            place = (place0 + origin).astype(jnp.float32)
            for i in range(SPAN):
                here = (place + float(i * GROUP)) * ((knots - 3) / plane) + 1.0
                for r in range(REACH):
                    j = knot0 + (i * GROUP * (knots - 3) // plane + r)
                    shapes[at_pair, i * REACH + r] = spline(here - j.astype(jnp.float32))
            row = lax.broadcasted_iota(jnp.int32, (SPOTS, LANES), 0)
            col = lax.broadcasted_iota(jnp.int32, (SPOTS, LANES), 1)
            spots[pl.ds(pl.multiple_of(at_pair * SPOTS, SUB), SPOTS), :] = (
                row + knot0 == col
            ).astype(jnp.float32)
            return 0

        lax.fori_loop(0, cap, shape, 0)

    for_pieces(
        order, comes, edge_in if wide else None,
        lambda side, c: direct(side, c).wait_recv(),
        lambda side, c: from_relay(side, c).wait_recv(),
    )
    each(tile_count, lambda step: head_copy(step, tile).wait_send())
    each(knot_count, lambda step: column_copy(step, knot).wait_send())
    for side in range(2):
        when(goes[side])(lambda side=side: tab_copy(side).wait_send())
    for_pieces(
        order, goes, edges,
        lambda side, c: direct(side, c).wait_send(),
        lambda side, c: to_relay(side, c).wait_send(),
    )
    if wide:
        for side in range(2):
            def passed(side=side):
                for c in range(CHUNKS):
                    from_relay(side, c).wait_send()

            when(relays[side])(passed)


def fill_field(groups, plane, knots, base, local, basis, store):
    for group in range(groups):
        first = group * GROUP * (knots - 3) // plane
        value = spread(local, first) * basis[group * WINDOW]
        for i in range(1, WINDOW):
            value += spread(local, first + i) * basis[group * WINDOW + i]
        store(group, value + base)


def refine_kernel(
    plane, tile_count, knot_count, block, cap,
    blocks, table, rigid, basis, weight, pull, image_sum, slope_sum, shapes, spots, bands, chosen,
    coef_in, local_in, penalty, local, own_out,
    field, coef, factors, system, work, marks, mine_first, mine_second, *share_refs,
):
    knots = 2 * block
    groups = plane // GROUP
    each = len(share_refs) // 3
    sets = [share_refs[n * each : (n + 1) * each] for n in range(3)]
    field[groups] = jnp.zeros((SUB, LANES), jnp.float32)
    base = shift_step * rigid[0].astype(jnp.float32)
    ones = jnp.ones((SUB, LANES), jnp.float32)
    local[...] = local_in[...]
    coef[...] = coef_in[...]
    holders = [[] for _ in range(knots)]
    for group in range(groups):
        first = group * GROUP * (knots - 3) // plane
        for i in range(WINDOW):
            if first + i < knots:
                holders[first + i].append((group, group * WINDOW + i))

    def store(group, value):
        field[group] = value

    def slabs():
        fill_field(groups, plane, knots, base, local, basis, store)
        for side in range(3):

            def body(m, _):
                pair = side * cap + m
                group = lax.shift_right_logical(table[0, side, m, 1], GROUP.bit_length() - 1)
                parts = [None] * SPOTS
                for i in range(SPAN):
                    here = pl.ds(i * SUB, SUB)
                    term = image_sum[pair, here, :] + slope_sum[pair, here, :] * field[group + i]
                    for r in range(REACH):
                        j = i * GROUP * (knots - 3) // plane + r
                        value = term * shapes[pair, i * REACH + r]
                        parts[j] = value if parts[j] is None else parts[j] + value
                zero = jnp.zeros((SUB, LANES), jnp.float32)
                parts = [zero if part is None else part for part in parts]
                for j in range(0, SPOTS, SUB):
                    marks[pl.ds(pl.multiple_of(pair * SPOTS + j, SUB), SUB), :] = row_sums(
                        parts[j : j + SUB]
                    )
                return 0

            lax.fori_loop(0, cap, body, 0)

    def gather(mine):
        for group in range(groups):
            here = slice(group * SUB, (group + 1) * SUB)
            field[group] = pull[here, :] + weight[here, :] * field[group]
        parts = []
        for j in range(knots):
            total = None
            for group, at in holders[j]:
                term = basis[at] * field[group]
                total = term if total is None else total + term
            parts.append(total)
        sums = jnp.concatenate(
            [row_sums(parts[j : j + SUB]) for j in range(0, knots, SUB)], axis=0
        )
        count = cap * SPOTS
        lines = []
        for side in range(3):
            at = slice(side * count, (side + 1) * count)
            values = lanes_dot(ones, marks[at, :])
            lines.append(
                -jnp.dot(
                    values, spots[at, :], precision=HIGHEST, preferred_element_type=jnp.float32
                )[0:1, :]
            )
        mine[0:1, :] = lanes_dot(ones, sums)[0:1, :] + lines[1]
        mine[1:2, :] = lines[0]
        mine[2:3, :] = lines[2]
        mine[3:SUB, :] = jnp.zeros((SUB - 3, LANES), jnp.float32)

    def solve(sums):
        own, lower, upper = sums[:, 0, :], sums[:, 1, :], sums[:, 2, :]
        none = jnp.zeros((1, LANES), jnp.float32)
        grads = (
            own
            + jnp.concatenate([lower[1:, :], none], axis=0)
            + jnp.concatenate([none, upper[:-1, :]], axis=0)
        )
        grad_sum = cols_dot(halves(grads, block), chosen[...])
        bend = jnp.dot(
            penalty[...], coef[...], precision=HIGHEST, preferred_element_type=jnp.float32
        )
        work[...] = -(grad_sum + smooth_weight * bend)
        forward = []
        for k in range(block):
            value = spread(work, k)
            for back in (3, 2, 1):
                if k >= back:
                    value = value - factors[back - 1, k] * forward[k - back]
            forward.append(value)
        steps = [None] * block
        for k in reversed(range(block)):
            value = forward[k] * factors[3, k]
            for ahead in (3, 2, 1):
                if k + ahead < block:
                    value = value - factors[ahead - 1, k + ahead] * steps[k + ahead]
            steps[k] = value
            work[k : k + 1, :] = value[0:1, :]
        coef[...] = coef[...] + work[...]
        spread_coef(blocks, coef[...], local)

    greet(tile_count, knot_count, slabs)
    band_knot, band_tile, band_table, band_finish = share(tile_count, knot_count, bands, sets[0])
    band_knot()
    open_knot, open_tile, arrived, finish_first = share(
        tile_count, knot_count, mine_first, sets[1]
    )
    gather(mine_first)
    open_knot()
    band_tile()
    open_tile()
    table_of = band_table()
    select = chosen[...]
    for d in range(BAND):
        system[d] = cols_dot(halves(table_of[:, d, :], block), select)
    factor(block, smoothing(block), system, factors)
    solve(arrived())
    slabs()
    gather(mine_second)
    open_knot, open_tile, arrived, finish_second = share(
        tile_count, knot_count, mine_second, sets[2]
    )
    open_knot()
    open_tile()
    solve(arrived())
    lane = lax.broadcasted_iota(jnp.int32, (SUB, LANES), 1)
    me = lax.axis_index("tile") * knot_count + lax.axis_index("knot")
    own_out[...] = lanes_dot((lane == me).astype(jnp.float32), coef[...])
    band_finish()
    finish_first()
    finish_second()


def warp_kernel(
    plane, knots, rigid, local, basis, image, slope, out, own_image, own_slope, field, load_sem, save_sem
):
    groups = plane // GROUP
    rows = plane // LANES
    part = rows // CUTS
    base = shift_step * rigid[0].astype(jnp.float32)

    def load(which, cut):
        src, dst = ((image, own_image), (slope, own_slope))[which]
        here = pl.ds(cut * part, part)
        return pltpu.make_async_copy(src.at[here], dst.at[here], load_sem.at[which, cut])

    def save(cut):
        here = pl.ds(cut * part, part)
        return pltpu.make_async_copy(own_image.at[here], out.at[here], save_sem.at[cut])

    for cut in range(CUTS):
        for which in range(2):
            load(which, cut).start()

    def store(group, value):
        field[group * SUB : (group + 1) * SUB, :] = value

    fill_field(groups, plane, knots, base, local, basis, store)
    for cut in range(CUTS):
        for which in range(2):
            load(which, cut).wait()

        def body(group, _):
            for r in range(SUB):
                row = group * SUB + r
                shift = jnp.broadcast_to(field[pl.ds(row, 1), :], (SUB, LANES))
                own_image[row] = own_image[row] + own_slope[row] * shift
            return 0

        lax.fori_loop(cut * (groups // CUTS), (cut + 1) * (groups // CUTS), body, 0, unroll=2)
        save(cut).start()
    for cut in range(CUTS):
        save(cut).wait()


def per_device(images, gradient, shifts, tile_blocks, intersections, start_coefficients):
    depth, plane = images.shape[1:]
    block = start_coefficients.shape[1]
    knots = 2 * block
    groups = plane // GROUP
    rows = plane // LANES
    padded = FRONT + rows + BACK
    tile_count = lax.axis_size("tile")
    knot_count = lax.axis_size("knot")
    cap = intersections.shape[2]
    side = math.isqrt(tile_count // 2)
    wide = 2 * side if side > 1 and 2 * side * side == tile_count else 0

    def flat(volume):
        return volume.reshape(depth, rows, LANES).transpose(1, 0, 2)

    image, slope = flat(images[0]), flat(gradient[0])
    volume = pltpu.VMEM((padded, SUB, LANES), jnp.float32)
    pair_of = pltpu.SemaphoreType.DMA((2,))
    piece_of = pltpu.SemaphoreType.DMA((2, 2 * CHUNKS))
    chunk_of = pltpu.SemaphoreType.DMA((CHUNKS,))

    basis, weight, pull, below, above, bands, chosen, coef, local, shapes, spots = pl.pallas_call(
        functools.partial(
            begin_kernel, depth, plane, block, tile_count, knot_count, cap, wide
        ),
        out_shape=(
            f32(groups * WINDOW, SUB, LANES),
            f32(rows, LANES),
            f32(rows, LANES),
            f32(rows, SUB, LANES),
            f32(rows, SUB, LANES),
            f32(SUB, LANES),
            f32(2 * tile_count, LANES),
            f32(block, LANES),
            f32(knots + SUB, LANES),
            f32(3 * cap, SPAN * REACH, SUB, LANES),
            f32(3 * cap * SPOTS, LANES),
        ),
        in_specs=[SMEM, SMEM, VMEM, ANY, ANY],
        out_specs=(VMEM,) * 3 + (ANY,) * 2 + (VMEM,) * 6,
        scratch_shapes=[
            pltpu.VMEM((rows, SUB, LANES), jnp.float32),
            pltpu.VMEM((rows, SUB, LANES), jnp.float32),
            pltpu.VMEM((rows // 2, SUB, LANES), jnp.float32),
            pltpu.VMEM((3, 2 * cap, LANES), jnp.float32),
            pltpu.VMEM((2, 2 * cap, LANES), jnp.float32),
            pltpu.VMEM((BAND, knots + SUB, SUB, LANES), jnp.float32),
            pltpu.VMEM((SUB, LANES), jnp.float32),
            pltpu.VMEM((tile_count, SUB, LANES), jnp.float32),
            pltpu.VMEM((knot_count, tile_count, SUB, LANES), jnp.float32),
            pair_of, pair_of, pair_of, piece_of, piece_of,
            chunk_of, chunk_of, chunk_of, chunk_of,
            pltpu.SemaphoreType.DMA((tile_count,)),
            pltpu.SemaphoreType.DMA((tile_count,)),
            pltpu.SemaphoreType.DMA((knot_count,)),
            pltpu.SemaphoreType.DMA((knot_count,)),
        ],
        compiler_params=pltpu.CompilerParams(
            collective_id=0, has_side_effects=True, vmem_limit_bytes=46 * 1024 * 1024
        ),
        name="begin",
    )(tile_blocks, intersections, start_coefficients, image, slope)
    image_sum, slope_sum = pl.pallas_call(
        functools.partial(pair_kernel, rows, cap),
        out_shape=(f32(3 * cap, SPAN * SUB, LANES),) * 2,
        in_specs=[SMEM] + [ANY] * 4,
        out_specs=(VMEM,) * 2,
        scratch_shapes=[volume] * 4 + [pltpu.SemaphoreType.DMA((4,))],
        compiler_params=pltpu.CompilerParams(vmem_limit_bytes=16 * 1024 * 1024),
        name="pairs",
    )(intersections, image, slope, below, above)
    penalty = jnp.asarray(smoothing(block))

    local, own = pl.pallas_call(
        functools.partial(refine_kernel, plane, tile_count, knot_count, block, cap),
        out_shape=(f32(knots + SUB, LANES), f32(SUB, block)),
        in_specs=[SMEM] * 3 + [VMEM] * 12,
        out_specs=(VMEM,) * 2,
        scratch_shapes=[
            pltpu.VMEM((groups + 1, SUB, LANES), jnp.float32),
            pltpu.VMEM((block, LANES), jnp.float32),
            pltpu.VMEM((4, block, SUB, LANES), jnp.float32),
            pltpu.VMEM((BAND, block, LANES), jnp.float32),
            pltpu.VMEM((block, LANES), jnp.float32),
            pltpu.VMEM((3 * cap * SPOTS, LANES), jnp.float32),
            pltpu.VMEM((SUB, LANES), jnp.float32),
            pltpu.VMEM((SUB, LANES), jnp.float32),
            *(share_scratch(tile_count, knot_count, SUB) * ITERS),
            *share_scratch(tile_count, knot_count, SUB),
        ],
        compiler_params=pltpu.CompilerParams(
            collective_id=1, has_side_effects=True, vmem_limit_bytes=24 * 1024 * 1024
        ),
        name="refine",
    )(
        tile_blocks, intersections, shifts, basis, weight, pull, image_sum, slope_sum, shapes,
        spots, bands, chosen, coef, local, penalty,
    )

    whole = pltpu.VMEM((rows, SUB, LANES), jnp.float32)
    warped = pl.pallas_call(
        functools.partial(warp_kernel, plane, knots),
        out_shape=f32(rows, depth, LANES),
        in_specs=[SMEM, VMEM, VMEM, ANY, ANY],
        out_specs=ANY,
        scratch_shapes=[
            whole,
            whole,
            pltpu.VMEM((rows, LANES), jnp.float32),
            pltpu.SemaphoreType.DMA((2, CUTS)),
            pltpu.SemaphoreType.DMA((CUTS,)),
        ],
        compiler_params=PARAMS,
        name="warp",
    )(shifts, local, basis, image, slope)
    return own[0:1], warped.transpose(1, 0, 2).reshape(1, depth, plane)


def solution(mesh):
    placed = (
        P("tile", "knot", None),
        P("tile", "knot", None),
        P("tile"),
        P("tile", None),
        P("tile", None, None, None),
        P(("tile", "knot"), None),
    )
    return jax.shard_map(
        per_device,
        mesh=mesh,
        in_specs=placed,
        out_specs=(P(("tile", "knot"), None), P("tile", "knot", None)),
        check_vma=False,
    )
```
